256 devices in a mesh: group: 2 (over core), dp: 8 (over z_lo, y), mp: 16 (over x, z_hi).
Axes of the slice: x: 4, y: 4, z: 8 (z_hi: 4, z_lo: 2; z = z_hi * 2 + z_lo), core: 2. Of those that a mesh axis runs over, the one named last changes fastest.
Arguments:
- contexts: bfloat16 [64, 4, 128, 8192], P(('group', 'dp'), None, None, 'mp'), may hold values from -6 to 6
- picks: int32 [64], P(('group', 'dp')), may hold values from 0 to 3
- teacher_out: bfloat16 [8192, 8192], P('mp'), may hold values from -0.0625 to 0.0625
- teacher_residual: bfloat16 [8192, 8192], P(('group', 'dp', 'mp')), may hold values from -200 to 200, as said below
- teacher_gain: float32 [8192], replicated, may hold values from 0.1 to 1.9
- student_hidden: bfloat16 [8192, 3584], P(('group', 'dp', 'mp')), may hold values from -700 to 700, as said below
- student_norm_gain: float32 [3584], replicated, may hold values from 0.1 to 1.9
- feature_map: bfloat16 [3584, 8192], P(('group', 'dp'), 'mp'), may hold values from -0.09375 to 0.09375
- positions: int32 [16, 512], P(('group', 'dp')), may hold values from 0 to 511, each once within a row
Outputs:
- grad_hidden: float32 [8192, 3584], P(('group', 'dp', 'mp'))
The draws below stay inside these ranges and needn't reach their ends.
Inputs may be any that keep to these rules, and one draw needn't show every extreme that they name: `picks`: the index of the picked response among the prompt's 4. `positions`: each row is a permutation of the tokens of its micro-batch. `teacher_residual`: real values. `student_hidden`: real values.
All inputs are finite; a program needn't handle non-finite values.
Results may differ from the reference program's by a relative error of at most 0.022.
Values may be sent and summed in bfloat16 or wider, within the bound.
No kernel may reach another device: no remote copies, remote signals or barrier semaphores. Data moves between devices by JAX's collectives and lax.ppermute only.
A program may use at most 128 MiB of HBM per device.

```python
import math
import jax
import jax.numpy as jnp
from jax import lax

DT = 8192
DS = 3584
NCAND = 4
RESP = 128
MICRO_TOKENS = 512
MBS = 16
TOKENS = 8192
PROMPTS = 64
N_MP = 16


def spread_scales(key, rows, cols):
    row_key, col_key, base_key = jax.random.split(key, 3)
    row_scale = jnp.exp(jax.random.uniform(row_key, (rows, 1), jnp.float32) * math.log(10.0))
    col_scale = jnp.exp(jax.random.uniform(col_key, (1, cols), jnp.float32) * math.log(10.0))
    return (row_scale, col_scale, base_key)


def draw_teacher_residual(key, part):
    key = jax.random.fold_in(key, 7)
    row_scale, col_scale, base_key = spread_scales(key, TOKENS, DT)
    trend = 3.0 ** (jnp.arange(DT, dtype=jnp.float32) / DT)
    base = jax.random.normal(base_key, (TOKENS, DT), jnp.float32)
    return (base * row_scale * col_scale * trend[None, :] * 0.1).astype(jnp.bfloat16)


def draw_student_hidden(key, part):
    key = jax.random.fold_in(key, 13)
    row_scale, col_scale, base_key = spread_scales(key, TOKENS, DS)
    base = jax.random.normal(base_key, (TOKENS, DS), jnp.float32)
    return (base * row_scale * col_scale).astype(jnp.bfloat16)


def place_ends(result, own_key, low, largest):
    longest = result.shape.index(max(result.shape))
    spots = []
    for shift in (0, 1):
        where = [jax.random.randint(jax.random.fold_in(own_key, axis), (), 0, length) for axis, length in enumerate(result.shape)]
        where[longest] = (where[longest] + shift) % result.shape[longest]
        spots.append(tuple(where))
    return result.at[spots[0]].set(low).at[spots[1]].set(largest)


def block_levels(stream_key, shape, shards, smallest, top_value):
    factor_of, own = 1.0, jax.random.fold_in(stream_key, 6)
    for dim, shards_of in shards:
        heights = jnp.exp(jax.random.uniform(jax.random.fold_in(own, dim), (shards_of,), jnp.float32, smallest / len(shards), top_value / len(shards)))
        factor_of = factor_of * jnp.repeat(heights, shape[dim] // shards_of).reshape([-1 if axis == dim else 1 for axis in range(len(shape))])
    return factor_of


def gaussian(stream_key, shape, spread, bound, shards=(), held_as=jnp.bfloat16):
    loudness = block_levels(stream_key, shape, shards, -0.22, 0.18) if shards else 1.0
    entries = jax.random.normal(stream_key, shape, jnp.float32) * spread * loudness
    return jnp.minimum(jnp.maximum(entries, -bound), bound).astype(held_as)


def setup_inputs(seed: int = 0) -> dict:
    streams_of = jax.random.split(jax.random.key(seed), 10)
    contexts = gaussian(streams_of[0], (PROMPTS, NCAND, RESP, DT), 1.0, 6.0, ((0, 16), (3, 16)))
    picks = place_ends(jax.random.randint(streams_of[1], (PROMPTS,), 0, NCAND), jax.random.fold_in(streams_of[1], 1), 0, NCAND - 1).astype(jnp.int32)
    teacher_out = gaussian(streams_of[2], (DT, DT), DT ** -0.5, 0.0625, ((0, 16),))
    teacher_residual = draw_teacher_residual(jax.random.fold_in(streams_of[9], 71), 0)
    teacher_gain = jnp.clip(1.0 + 0.18 * jax.random.normal(streams_of[4], (DT,), jnp.float32), 0.1, 1.9)
    student_hidden = draw_student_hidden(jax.random.fold_in(streams_of[9], 71), 0)
    student_norm_gain = jnp.clip(1.0 + 0.18 * jax.random.normal(streams_of[6], (DS,), jnp.float32), 0.1, 1.9)
    feature_map = gaussian(streams_of[7], (DS, DT), DS ** -0.5, 0.09375, ((0, 16), (1, 16)))
    positions = jax.vmap(lambda own: jax.random.permutation(own, MICRO_TOKENS))(jax.random.split(streams_of[8], MBS)).reshape((MBS, MICRO_TOKENS)).astype(jnp.int32)
    return {"contexts": contexts, "picks": picks, "teacher_out": teacher_out, "teacher_residual": teacher_residual, "teacher_gain": teacher_gain, "student_hidden": student_hidden, "student_norm_gain": student_norm_gain, "feature_map": feature_map, "positions": positions}


eps = 1e-06

def reference(contexts, picks, teacher_out, teacher_residual, teacher_gain, student_hidden, student_norm_gain, feature_map, positions):
    picked = jnp.take_along_axis(contexts, picks[:, None, None, None], axis=1)[:, 0]
    picked = picked.reshape(MBS, MICRO_TOKENS, DT)
    resid = teacher_residual.reshape(MBS, MICRO_TOKENS, DT)
    block = DT // N_MP
    weights = teacher_out.astype(jnp.float32)

    def teach(pair):
        rows, res = pair
        rows = rows.astype(jnp.float32)
        total = jnp.zeros((MICRO_TOKENS, DT), jnp.float32)
        for shard in range(N_MP):
            part = jnp.dot(rows[:, shard * block:(shard + 1) * block], weights[shard * block:(shard + 1) * block], preferred_element_type=jnp.float32)
            part = lax.optimization_barrier(part.astype(jnp.bfloat16))
            total = total + part.astype(jnp.float32)
        pre = total + res.astype(jnp.float32)
        stat = lax.optimization_barrier(jnp.mean(pre * pre, axis=1, keepdims=True))
        return (pre * lax.rsqrt(stat + eps) * teacher_gain).astype(jnp.bfloat16)
    target = lax.map(teach, (picked, resid))
    aligned = jnp.take_along_axis(target, positions[:, :, None], axis=1).reshape(TOKENS, DT)
    hidden_rows = student_hidden.astype(jnp.float32)
    inverse_deviation = lax.rsqrt(lax.optimization_barrier(jnp.mean(hidden_rows * hidden_rows, axis=1, keepdims=True)) + eps)
    centered_unit = hidden_rows * inverse_deviation
    normalized_rows = (centered_unit * student_norm_gain).astype(jnp.bfloat16)
    mapping = feature_map.astype(jnp.float32)
    mapped = jnp.dot(normalized_rows.astype(jnp.float32), mapping, preferred_element_type=jnp.float32)
    error = (mapped - aligned.astype(jnp.float32)).astype(jnp.bfloat16).astype(jnp.float32)
    back = jnp.zeros((TOKENS, DS), jnp.float32)
    for shard in range(N_MP):
        part = jnp.dot(error[:, shard * block:(shard + 1) * block], mapping[:, shard * block:(shard + 1) * block].T, preferred_element_type=jnp.float32)
        part = lax.optimization_barrier(part.astype(jnp.bfloat16))
        back = back + part.astype(jnp.float32)
    gained_rows = back * student_norm_gain
    return inverse_deviation * (gained_rows - centered_unit * lax.optimization_barrier(jnp.mean(gained_rows * centered_unit, axis=1, keepdims=True)))
```

```python
import jax
import jax.numpy as jnp
from jax import lax
from jax.sharding import Mesh, PartitionSpec as P

eps = 1e-06
f32, bf16 = jnp.float32, jnp.bfloat16


def shift(a, axis, by):
    n = 4
    return lax.ppermute(a, axis, [(i, (i + by) % n) for i in range(n)])


def dot(a, b):
    return jnp.dot(a, b, preferred_element_type=f32)


def block(a, index, size, axis):
    return lax.dynamic_slice_in_dim(a, index * size, size, axis)


def shards(
    contexts,
    picks,
    teacher_out,
    teacher_residual,
    teacher_gain,
    student_hidden,
    student_norm_gain,
    feature_map,
    positions,
):
    prompts, _, resp, depth = contexts.shape
    tokens = prompts * resp
    width = teacher_out.shape[1]
    cols = width // 4
    half = cols // 2
    rows = student_hidden.shape[0]
    d_student = student_hidden.shape[1]
    x, z, g = lax.axis_index("x"), lax.axis_index("zh"), lax.axis_index("group")

    own_map = lax.all_gather(feature_map, ("zh", "zl", "y"), axis=0, tiled=True)
    other_map = lax.ppermute(own_map, "group", [(0, 1), (1, 0)])
    own_map = own_map.reshape(4, d_student // 2, -1)
    other_map = other_map.reshape(4, d_student // 2, -1)

    hidden = student_hidden.astype(f32)
    rstd = lax.rsqrt(jnp.mean(hidden * hidden, axis=1, keepdims=True) + eps)
    xhat = hidden * rstd
    normed = (xhat * student_norm_gain).astype(bf16)
    came = [normed] + [shift(normed, "x", k) for k in (1, 2, 3)]
    ring = jnp.concatenate([came[3], came[2], came[1], came[0]] * 2, axis=0)
    every = lax.dynamic_slice_in_dim(ring, (3 - x) * rows, 4 * rows, 0)

    table = jnp.concatenate(
        [block(teacher_residual, x, cols, 1)]
        + [
            shift(block(teacher_residual, (x + k) % 4, cols, 1), "x", k)
            for k in (1, 2, 3)
        ],
        axis=0,
    )
    slot = jnp.arange(4 * rows)
    table_row = (((x - slot // rows) % 4) * 4 + z) * rows + slot % rows

    picked = jnp.concatenate(
        [lax.dynamic_index_in_dim(contexts[p], picks[p], 0, False) for p in range(prompts)],
        axis=0,
    )
    places = positions.reshape(4, 4, rows)
    weights = [block(teacher_out, (x + k) % 4, cols, 1) for k in range(4)]

    def reduced(by):
        want = lax.dynamic_index_in_dim(places, (z + by) % 4, 1, False).reshape(-1, 1)
        choose = (want == jnp.arange(tokens)[None, :]).astype(bf16)
        part = dot(choose, picked).astype(bf16)
        far = dot(part, weights[2]).astype(bf16)
        far_up = shift(far[:, :half], "x", 1)
        far_down = shift(far[:, half:], "x", -1)
        up = dot(part, weights[1])
        up = jnp.concatenate([up[:, :half] + far_up.astype(f32), up[:, half:]], axis=1)
        down = dot(part, weights[3])
        down = jnp.concatenate([down[:, :half], down[:, half:] + far_down.astype(f32)], axis=1)
        from_down = shift(up.astype(bf16), "x", 1)
        from_up = shift(down.astype(bf16), "x", -1)
        place = (want == table_row[None, :]).astype(bf16)
        own = dot(part, weights[0]) + dot(place, table)
        return own + from_down.astype(f32) + from_up.astype(f32)

    far = reduced(2).astype(bf16)
    far_up = shift(far[:, :half], "zh", 1)
    far_down = shift(far[:, half:], "zh", -1)
    up = reduced(1)
    up = jnp.concatenate([up[:, :half] + far_up.astype(f32), up[:, half:]], axis=1)
    from_down = shift(up.astype(bf16), "zh", 1)
    down = reduced(3)
    down = jnp.concatenate([down[:, :half], down[:, half:] + far_down.astype(f32)], axis=1)
    from_up = shift(down.astype(bf16), "zh", -1)
    pre = reduced(0) + from_down.astype(f32) + from_up.astype(f32)

    square = jnp.sum(pre * pre, axis=1, keepdims=True)
    total = square + shift(square, "x", 1) + shift(square, "x", 2) + shift(square, "x", 3)
    inverse = lax.rsqrt(total / width + eps)
    aligned = (pre * inverse * block(teacher_gain, x, cols, 0)).astype(bf16)

    d_half = d_student // 2
    own_every, other_every = block(every, g, d_half, 1), block(every, 1 - g, d_half, 1)
    mapped = jnp.concatenate(
        [dot(own_every, own_map[c]) + dot(other_every, other_map[c]) for c in range(4)],
        axis=1,
    )
    error = (mapped - aligned.astype(f32)).astype(bf16)
    errors = jnp.split(error, 4, axis=1)

    def back_of(maps):
        return sum(
            lax.dot_general(
                errors[c], maps[c], (((1,), (1,)), ((), ())), preferred_element_type=f32
            )
            for c in range(4)
        )

    own_back, other_back = back_of(own_map), back_of(other_map)
    first = jnp.where(g == 0, own_back, other_back)
    second = jnp.where(g == 0, other_back, own_back)
    back = jnp.concatenate([first, second], axis=1).astype(bf16)
    summed = block(back, x, rows, 0).astype(f32)
    for k in (1, 2, 3):
        summed += shift(block(back, (x + k) % 4, rows, 0), "x", k).astype(f32)
    scaled = summed * student_norm_gain
    return rstd * (scaled - xhat * jnp.mean(scaled * xhat, axis=1, keepdims=True))


def solution(mesh):
    axes = ("group", "zl", "y", "x", "zh")
    fine = Mesh(mesh.devices.reshape(2, 2, 4, 4, 4), axes)
    gd, mp = ("group", "zl", "y"), ("x", "zh")
    in_specs = (
        P(gd, None, None, mp),
        P(gd),
        P(mp, None),
        P(axes, None),
        P(),
        P(axes, None),
        P(),
        P(gd, mp),
        P(gd, None),
    )
    return jax.shard_map(
        shards, mesh=fine, in_specs=in_specs, out_specs=P(axes, None), check_vma=False
    )
```

```python
import functools
import jax
import jax.numpy as jnp
from jax import lax
from jax.experimental import pallas as pl
from jax.experimental.pallas import tpu as pltpu
from jax.sharding import Mesh, PartitionSpec as P

eps = 1e-06
f32, bf16 = jnp.float32, jnp.bfloat16
VMEM = pl.BlockSpec(memory_space=pltpu.VMEM)
SMEM = pl.BlockSpec(memory_space=pltpu.SMEM)
ANY = pl.BlockSpec(memory_space=pl.ANY)
DMA = pltpu.SemaphoreType.DMA
OFFSETS = (2, 1, 3, 0)
PAIRS = (((0, 0, 2), (0, 1, 2)), ((1, 0, 1), (2, 0, 1)), ((3, 0, 2), (3, 1, 2)))


def shift(a, axis, by):
    return lax.ppermute(a, axis, [(i, (i + by) % 4) for i in range(4)])


def across(a, kind):
    return lax.ppermute(a, "x", [(i, 3 - i if kind else i ^ 1) for i in range(4)])


def partner(x, kind):
    return 3 - x if kind else x + 1 - 2 * lax.rem(x, 2)


def dot(a, b):
    return jnp.dot(a, b, preferred_element_type=f32)


def call(body, outs, ins, specs, scratch=(), name=None, aliases=None, out_spec=VMEM, limit=56):
    return pl.pallas_call(
        body,
        out_shape=[jax.ShapeDtypeStruct(s, t) for s, t in outs],
        in_specs=specs,
        out_specs=[out_spec] * len(outs),
        scratch_shapes=list(scratch),
        compiler_params=pltpu.CompilerParams(vmem_limit_bytes=limit * 1024 * 1024),
        cost_estimate=pl.CostEstimate(flops=1, bytes_accessed=1, transcendentals=0),
        input_output_aliases=aliases or {},
        name=name,
    )(*ins)


def gate(a, token):
    return call(
        lambda a_ref, t_ref, o_ref: None,
        [(a.shape, a.dtype)],
        [a, token],
        [ANY, ANY],
        name="gate",
        aliases={0: 0},
        out_spec=ANY,
    )[0]


def column(w_ref, index, cols, buf, sem):
    start = pl.multiple_of(index * cols, cols)
    return pltpu.make_async_copy(w_ref.at[:, pl.ds(start, cols)], buf, sem)


def chunk(part_ref, where):
    q, at, of = where
    n = part_ref.shape[1] // of
    return part_ref[q, at * n : (at + 1) * n, :]


def prep_body(residual, *outs):
    x = lax.axis_index("x")
    cols = residual.shape[1] // 4
    for k, out in enumerate(outs):
        start = pl.multiple_of(lax.rem(x + k, 4) * cols, cols)
        out[...] = residual[:, pl.ds(start, cols)]


def norm_body(hidden, gain, token, out):
    rows = hidden[...].astype(f32)
    rstd = lax.rsqrt(jnp.mean(rows * rows, axis=1, keepdims=True) + eps)
    out[...] = (rows * rstd * gain[...]).astype(bf16)


def merge_body(*refs):
    x = lax.axis_index("x")
    every = refs[-1]
    rows = refs[0].shape[0]
    for k in range(4):
        start = pl.multiple_of(lax.rem(x + 4 - k, 4) * rows, rows)
        every[pl.ds(start, rows), :] = refs[k][...]


def send_blocks(part_ref, pair, wbuf, copies, outs, at_row):
    for kind in range(2):
        rows = chunk(part_ref, pair[kind])
        for h in range(2):
            if copies:
                copies[kind][h].wait()
            cols = wbuf.shape[-1]
            tile = cols // 4
            for c in range(4):
                at = slice(c * tile, (c + 1) * tile)
                out = dot(rows, wbuf[kind, h, :, at])
                to = slice(at_row, at_row + rows.shape[0])
                outs[kind][to, h * cols + c * tile : h * cols + (c + 1) * tile] = out.astype(bf16)


def send_copies(w_ref, wbuf, sems, cols):
    x = lax.axis_index("x")
    copies = []
    for kind in range(2):
        p = partner(x, kind)
        copies.append(
            [column(w_ref, b, cols, wbuf.at[kind, h], sems.at[kind, h]) for h, b in enumerate((p, partner(p, 1 - kind)))]
        )
        for c in copies[-1]:
            c.start()
    return copies


def select_body(sizes, ctx_ref, picks_ref, pos_ref, w_ref, *refs):
    refs = refs[5:]
    prompts, resp, rows, cols = sizes
    part_ref, place_ref, out_a, out_b, picked, nat, wbuf, sems, wsems = refs
    x, z = lax.axis_index("x"), lax.axis_index("zh")
    tokens = prompts * resp
    copies = []
    for p in range(prompts):
        copies.append(
            pltpu.make_async_copy(
                ctx_ref.at[p, picks_ref[p]], picked.at[pl.ds(p * resp, resp), :], sems.at[p]
            )
        )
        copies[-1].start()
    wcopies = send_copies(w_ref, wbuf, wsems, cols)
    lanes = min(128, tokens)
    want = jnp.broadcast_to(pos_ref[...], (lanes, tokens)).T
    lane = lax.broadcasted_iota(jnp.int32, (tokens, lanes), 1)
    chooses = [(want == lane + c * lanes).astype(bf16) for c in range(tokens // lanes)]
    slot = lax.broadcasted_iota(jnp.int32, (tokens, 4 * rows), 1)
    row = (lax.rem(x - slot // rows + 4, 4) * 4 + z) * rows + lax.rem(slot, rows)
    place = (want[:, : 4 * rows] == row).astype(f32)
    for c in copies:
        c.wait()
    nat[...] = dot(jnp.concatenate(chooses, axis=1), picked[...])
    for q, by in enumerate(OFFSETS):
        zq = lax.rem(z + by, 4)
        for k in range(4):
            at = pl.ds(pl.multiple_of(k * 4 * rows + zq * rows, rows), rows)
            part_ref[q, k * rows : (k + 1) * rows, :] = nat[at, :].astype(bf16)
    nat[:, : 4 * rows] = place
    for q, by in enumerate(OFFSETS):
        zq = lax.rem(z + by, 4)
        for k in range(4):
            at = pl.ds(pl.multiple_of(k * 4 * rows + zq * rows, rows), rows)
            place_ref[q, k * rows : (k + 1) * rows, :] = nat[at, : 4 * rows].astype(bf16)
    send_blocks(part_ref, PAIRS[0], wbuf, wcopies, (out_a, out_b), 0)
    send_blocks(part_ref, PAIRS[1], wbuf, None, (out_a, out_b), 2 * rows)


def more_body(pair, part_ref, w_ref, *refs):
    out_a, out_b, wbuf, wsems = refs[-4:]
    copies = send_copies(w_ref, wbuf, wsems, out_a.shape[1] // 2)
    send_blocks(part_ref, pair, wbuf, copies, (out_a, out_b), 0)


def mid_body(pair, row, part_ref, w_ref, in_a, in_b, *refs):
    out_a, out_b, wbuf, sems = refs[-4:]
    x = lax.axis_index("x")
    cols = out_a.shape[1]
    copies = [column(w_ref, partner(x, 1 - k), cols, wbuf.at[k], sems.at[k]) for k in range(2)]
    for c in copies:
        c.start()
    tile = cols // 4
    for kind, (came, to) in enumerate(((in_a, out_a), (in_b, out_b))):
        rows = chunk(part_ref, pair[kind])
        here = slice(row, row + rows.shape[0])
        copies[kind].wait()
        for c in range(4):
            at = slice(c * tile, (c + 1) * tile)
            out = dot(rows, wbuf[kind, :, at])
            out += came[here, cols + c * tile : cols + (c + 1) * tile].astype(f32)
            to[:, at] = out.astype(bf16)


def own_body(stage, part_ref, place_ref, w_ref, t0, t1, t2, t3, a1, b1, a2, b2, *refs):
    wbuf, sem = refs[-2:]
    x = lax.axis_index("x")
    cols = t0.shape[1]
    wcopy = column(w_ref, x, cols, wbuf, sem)
    wcopy.start()
    wcopy.wait()
    tile = cols // 4
    for kind, (first, second) in enumerate(((a1, a2), (b1, b2))):
        _, at, of = PAIRS[stage][kind]
        rows = chunk(part_ref, PAIRS[stage][kind])
        place = chunk(place_ref, PAIRS[stage][kind])
        n = rows.shape[0]
        row = 2 * n // 4 if stage == 1 else 0
        came = slice(row, row + n)
        square = jnp.zeros((n, 1), f32)
        here = slice(at * n, (at + 1) * n)
        for c in range(4):
            cs = slice(c * tile, (c + 1) * tile)
            near = slice((c % 2) * tile, (c % 2 + 1) * tile)
            table = jnp.concatenate([t[:, cs] for t in (t0, t1, t2, t3)], axis=0)
            out = dot(rows, wbuf[:, cs]) + dot(place, table)
            out += first[came, cs].astype(f32) + second[:, cs].astype(f32)
            if stage == 0:
                refs[-4 + c // 2][here, near] = out.astype(bf16)
            elif stage == 1:
                if kind == c // 2:
                    out += refs[kind][:, near].astype(f32)
                refs[-4 + kind][:, cs] = out.astype(bf16)
            else:
                out += refs[0][here, cs].astype(f32) + refs[1][here, cs].astype(f32)
                refs[-4][here, cs] = out
                square += jnp.sum(out * out, axis=1, keepdims=True)
        if stage == 2:
            refs[-3][here, :] = square


def map_body(accumulate, every, half, maps, *refs):
    g = lax.axis_index("group")
    out = refs[-1]
    width = every.shape[1] // 2
    which = g if half == 0 else 1 - g
    rows = every[:, pl.ds(pl.multiple_of(which * width, width), width)]
    got = dot(rows, maps[...])
    out[...] = got + refs[0][...] if accumulate else got


def mapped_half(every, maps, half, before=None):
    tok, cols = every.shape[0], maps.shape[1]
    d_half = every.shape[1] // 2
    blocks = pl.BlockSpec((tok, cols), lambda c: (0, c))
    return pl.pallas_call(
        lambda e, m, *r: map_body(before is not None, e, half, m, *r),
        grid=(4,),
        out_shape=jax.ShapeDtypeStruct((tok, 4 * cols), f32),
        in_specs=[
            pl.BlockSpec(every.shape, lambda c: (0, 0)),
            pl.BlockSpec((d_half, cols), lambda c: (c, 0)),
        ]
        + ([blocks] if before is not None else []),
        out_specs=blocks,
        compiler_params=pltpu.CompilerParams(vmem_limit_bytes=40 * 1024 * 1024),
        cost_estimate=pl.CostEstimate(flops=1, bytes_accessed=1, transcendentals=0),
        name=f"mapped{half}",
    )(every, maps, *([before] if before is not None else []))


def back_body(mapped, pre, gain, s0, s1, s2, s3, own_map, other_map, *refs):
    outs, acc = refs[:4], refs[4]
    c = pl.program_id(0)
    x, g = lax.axis_index("x"), lax.axis_index("group")
    rows = outs[0].shape[0]
    d_half = own_map.shape[0]
    total = s0[...] + s1[...] + s2[...] + s3[...]
    inverse = lax.rsqrt(total / (4 * 4 * mapped.shape[1]) + eps)
    aligned = (pre[...] * inverse * gain[...]).astype(bf16)
    error = (mapped[...] - aligned.astype(f32)).astype(bf16)

    @pl.when(c == 0)
    def _():
        acc[...] = jnp.zeros_like(acc)

    for which, maps in ((g, own_map), (1 - g, other_map)):
        at = pl.ds(pl.multiple_of(which * d_half, d_half), d_half)
        acc[:, at] += lax.dot_general(
            error, maps[...], (((1,), (1,)), ((), ())), preferred_element_type=f32
        )

    @pl.when(c == pl.num_programs(0) - 1)
    def _():
        for k, out in enumerate(outs):
            start = pl.multiple_of(lax.rem(x + k, 4) * rows, rows)
            out[...] = acc[pl.ds(start, rows), :].astype(bf16)


def back_blocks(mapped, pre, gain, squares, own_map, other_map, d_student):
    tok, cols = mapped.shape[0], own_map.shape[1]
    blocks = pl.BlockSpec((tok, cols), lambda c: (0, c))
    maps = pl.BlockSpec((d_student // 2, cols), lambda c: (c, 0))
    x = lax.axis_index("x")
    gain = lax.dynamic_slice_in_dim(gain, x * 4 * cols, 4 * cols, 0).reshape(1, -1)
    return pl.pallas_call(
        back_body,
        grid=(4,),
        out_shape=[jax.ShapeDtypeStruct((tok // 4, d_student), bf16)] * 4,
        in_specs=[blocks, blocks, pl.BlockSpec((1, cols), lambda c: (0, c))]
        + [pl.BlockSpec((tok, 1), lambda c: (0, 0))] * 4
        + [maps, maps],
        out_specs=[pl.BlockSpec((tok // 4, d_student), lambda c: (0, 0))] * 4,
        scratch_shapes=[pltpu.VMEM((tok, d_student), f32)],
        compiler_params=pltpu.CompilerParams(vmem_limit_bytes=40 * 1024 * 1024),
        cost_estimate=pl.CostEstimate(flops=1, bytes_accessed=1, transcendentals=0),
        name="back",
    )(mapped, pre, gain, *squares, own_map, other_map)


def final_body(hidden, gain, p0, p1, p2, p3, out):
    rows = hidden[...].astype(f32)
    rstd = lax.rsqrt(jnp.mean(rows * rows, axis=1, keepdims=True) + eps)
    xhat = rows * rstd
    summed = (p0[...].astype(f32) + p1[...].astype(f32)) + (p2[...].astype(f32) + p3[...].astype(f32))
    scaled = summed * gain[...]
    out[...] = rstd * (scaled - xhat * jnp.mean(scaled * xhat, axis=1, keepdims=True))


def shards(
    contexts,
    picks,
    teacher_out,
    teacher_residual,
    teacher_gain,
    student_hidden,
    student_norm_gain,
    feature_map,
    positions,
):
    prompts, _, resp, depth = contexts.shape
    cols = teacher_out.shape[1] // 4
    rows, d_student = student_hidden.shape
    tok = 4 * rows
    gain_row = student_norm_gain.reshape(1, -1)

    own_map = lax.all_gather(feature_map, ("zh", "zl", "y"), axis=0, tiled=True)

    prepared = call(
        prep_body,
        [((rows, cols), bf16)] * 4,
        [teacher_residual],
        [VMEM],
        name="prep",
    )
    table = [prepared[0]] + [shift(prepared[k], "x", k) for k in (1, 2, 3)]
    normed = call(
        norm_body, [((rows, d_student), bf16)], [student_hidden, gain_row, prepared[0]], [VMEM, VMEM, ANY], name="norm"
    )[0]

    part, place, *sent = call(
        functools.partial(select_body, (prompts, resp, rows, cols)),
        [((4, tok, depth), bf16), ((4, tok, tok), bf16)] + [((tok * 3 // 2, 2 * cols), bf16)] * 2,
        [contexts, picks, positions, teacher_out, normed, *table],
        [ANY, SMEM, VMEM, ANY] + [ANY] * 5,
        [
            pltpu.VMEM((prompts * resp, depth), bf16),
            pltpu.VMEM((prompts * resp, depth), f32),
            pltpu.VMEM((2, 2, depth, cols), bf16),
            DMA((prompts,)),
            DMA((2, 2)),
        ],
        name="select",
    )
    first = [[across(sent[k], k) for k in range(2)]] * 2

    def more(i, n, *tokens):
        outs = call(
            functools.partial(more_body, PAIRS[i]),
            [((n, 2 * cols), bf16)] * 2,
            [part, teacher_out, *tokens],
            [VMEM, ANY] + [ANY] * len(tokens),
            [pltpu.VMEM((2, 2, depth, cols), bf16), DMA((2, 2))],
            name=f"more{i}",
        )
        first.append([across(outs[k], k) for k in range(2)])
        return outs[0]

    every = call(
        merge_body,
        [((tok, d_student), bf16)],
        [normed] + [shift(normed, "x", k) for k in (1, 2, 3)],
        [VMEM] * 4,
        name="merge",
    )[0]

    def mid(i, *tokens):
        n = tok // PAIRS[i][0][2]
        outs = call(
            functools.partial(mid_body, PAIRS[i], tok // 2 if i == 1 else 0),
            [((n, cols), bf16)] * 2,
            [part, teacher_out, *first[i], *tokens],
            [VMEM, ANY, VMEM, VMEM] + [ANY] * len(tokens),
            [pltpu.VMEM((2, depth, cols), bf16), DMA((2,))],
            name=f"mid{i}",
        )
        return outs[0], [across(outs[k], 1 - k) for k in range(2)]

    def own(i, second, extra, outs, *tokens):
        return call(
            functools.partial(own_body, i),
            outs,
            [part, place, teacher_out, *table, *first[i], *second, *extra, *tokens],
            [VMEM, VMEM, ANY] + [VMEM] * (8 + len(extra)) + [ANY] * len(tokens),
            [pltpu.VMEM((depth, cols), bf16), DMA],
            name=f"own{i}",
        )

    t, second0 = mid(0)
    t, second1 = mid(1, t, every)
    far = own(0, second0, (), [((tok, cols // 2), bf16)] * 2, t)
    far_z = shift(far[0], "zh", 1), shift(far[1], "zh", -1)
    near = own(1, second1, far_z, [((tok, cols), bf16)] * 2)
    near_z = shift(near[0], "zh", 1), shift(near[1], "zh", -1)
    t = more(2, tok // 2, near[0])
    t, second2 = mid(2, t)
    pre, square = own(2, second2, near_z, [((tok, cols), f32), ((tok, 1), f32)], t)
    own_map = gate(own_map, square)
    other_map = lax.ppermute(own_map, "group", [(0, 1), (1, 0)])
    mapped = mapped_half(every, own_map, 0)
    squares = [square] + [shift(square, "x", k) for k in (1, 2, 3)]
    mapped = mapped_half(every, other_map, 1, mapped)
    backs = back_blocks(mapped, pre, teacher_gain, squares, own_map, other_map, d_student)
    parts = [backs[0]] + [shift(backs[k], "x", k) for k in (1, 2, 3)]
    return call(
        final_body,
        [((rows, d_student), f32)],
        [student_hidden, gain_row, *parts],
        [VMEM] * 6,
        name="final",
    )[0]


def solution(mesh):
    axes = ("group", "zl", "y", "x", "zh")
    fine = Mesh(mesh.devices.reshape(2, 2, 4, 4, 4), axes)
    gd, mp = ("group", "zl", "y"), ("x", "zh")
    in_specs = (
        P(gd, None, None, mp),
        P(gd),
        P(mp, None),
        P(axes, None),
        P(),
        P(axes, None),
        P(),
        P(gd, mp),
        P(gd, None),
    )
    return jax.shard_map(
        shards, mesh=fine, in_specs=in_specs, out_specs=P(axes, None), check_vma=False
    )
```

```python
import functools
import jax
import jax.numpy as jnp
from jax import lax
from jax.experimental import pallas as pl
from jax.experimental.pallas import tpu as pltpu
from jax.sharding import Mesh, PartitionSpec as P

eps = 1e-06
f32, bf16 = jnp.float32, jnp.bfloat16
VMEM = pl.BlockSpec(memory_space=pltpu.VMEM)
SMEM = pl.BlockSpec(memory_space=pltpu.SMEM)
ANY = pl.BlockSpec(memory_space=pl.ANY)
HBM = pl.BlockSpec(memory_space=pltpu.HBM)
DMA = pltpu.SemaphoreType.DMA
OFFSETS = (2, 1, 3, 0)
PAIRS = (((0, 0, 2), (0, 1, 2)), ((1, 0, 1), (2, 0, 1)), ((3, 0, 2), (3, 1, 2)))


def shift(a, axis, by):
    return lax.ppermute(a, axis, [(i, (i + by) % 4) for i in range(4)])


def across(a, kind):
    return lax.ppermute(a, "x", [(i, 3 - i if kind else i ^ 1) for i in range(4)])


def partner(x, kind):
    return 3 - x if kind else x + 1 - 2 * lax.rem(x, 2)


def dot(a, b):
    return jnp.dot(a, b, preferred_element_type=f32)


def call(body, outs, ins, specs, scratch=(), name=None, aliases=None, out_spec=VMEM, limit=20, moved=1):
    return pl.pallas_call(
        body,
        out_shape=[jax.ShapeDtypeStruct(s, t) for s, t in outs],
        in_specs=specs,
        out_specs=[out_spec] * len(outs),
        scratch_shapes=list(scratch),
        compiler_params=pltpu.CompilerParams(vmem_limit_bytes=limit * 1024 * 1024),
        cost_estimate=pl.CostEstimate(flops=1, bytes_accessed=moved, transcendentals=0),
        input_output_aliases=aliases or {},
        name=name,
    )(*ins)


def gate(a, *tokens):
    return call(
        lambda *refs: None,
        [(a.shape, a.dtype)],
        [a, *tokens],
        [ANY] * (1 + len(tokens)),
        name="gate",
        aliases={0: 0},
        out_spec=ANY,
    )[0]


def column(w_ref, index, cols, buf, sem):
    start = pl.multiple_of(index * cols, cols)
    return pltpu.make_async_copy(w_ref.at[:, pl.ds(start, cols)], buf, sem)


def chunk(part_ref, where):
    q, at, of = where
    n = part_ref.shape[1] // of
    return part_ref[q, at * n : (at + 1) * n, :]


def prep_body(residual, *outs):
    x = lax.axis_index("x")
    cols = residual.shape[1] // 4
    for k, out in enumerate(outs):
        start = pl.multiple_of(lax.rem(x + k, 4) * cols, cols)
        out[...] = residual[:, pl.ds(start, cols)]


def norm_body(hidden, gain, *refs):
    out = refs[-1]
    rows = hidden[...].astype(f32)
    rstd = lax.rsqrt(jnp.mean(rows * rows, axis=1, keepdims=True) + eps)
    out[...] = (rows * rstd * gain[...][None, :]).astype(bf16)


def merge_body(low_of, mine, came, *refs):
    out = refs[-1]
    n = mine.shape[0]
    low = low_of(lax.axis_index("x"))
    out[pl.ds(pl.multiple_of(low * n, n), n), :] = mine[...]
    out[pl.ds(pl.multiple_of((1 - low) * n, n), n), :] = came[...]


def send_blocks(part_ref, pair, wbuf, copies, outs):
    cols = wbuf.shape[-1]
    tile = cols // 4
    for kind in range(2):
        rows = chunk(part_ref, pair[kind])
        n = outs[kind][0].shape[0]
        for h in range(2):
            if copies:
                copies[kind][h].wait()
            for c in range(4):
                out = dot(rows, wbuf[kind, h, :, c * tile : (c + 1) * tile]).astype(bf16)
                for i, to in enumerate(outs[kind]):
                    to[:, h * cols + c * tile : h * cols + (c + 1) * tile] = out[i * n : (i + 1) * n]


def stacked(pieces, cs):
    return jnp.concatenate([r[:, cs].astype(f32) for r in pieces], axis=0)


def send_copies(w_ref, wbuf, sems, cols):
    x = lax.axis_index("x")
    copies = []
    for kind in range(2):
        p = partner(x, kind)
        copies.append(
            [column(w_ref, b, cols, wbuf.at[kind, h], sems.at[kind, h]) for h, b in enumerate((p, partner(p, 1 - kind)))]
        )
        for c in copies[-1]:
            c.start()
    return copies


def pick_body(sizes, ctx_ref, picks_ref, pos_ref, w_ref, token, part_ref, place_ref, w_out, picked, nat, sems):
    prompts, resp, rows = sizes
    x, z = lax.axis_index("x"), lax.axis_index("zh")
    tokens = prompts * resp
    copies = []
    for p in range(prompts):
        copies.append(
            pltpu.make_async_copy(
                ctx_ref.at[p, picks_ref[p]], picked.at[pl.ds(p * resp, resp), :], sems.at[p]
            )
        )
        copies[-1].start()
    wcopy = pltpu.make_async_copy(w_ref, w_out, sems.at[prompts])
    wcopy.start()
    lanes = min(128, tokens)
    want = jnp.broadcast_to(pos_ref[...], (lanes, tokens)).T
    lane = lax.broadcasted_iota(jnp.int32, (tokens, lanes), 1)
    chooses = [(want == lane + c * lanes).astype(bf16) for c in range(tokens // lanes)]
    slot = lax.broadcasted_iota(jnp.int32, (tokens, 4 * rows), 1)
    row = (lax.rem(x - slot // rows + 4, 4) * 4 + z) * rows + lax.rem(slot, rows)
    nat[:, : 4 * rows] = (want[:, : 4 * rows] == row).astype(f32)

    def sort(to, width):
        for q, by in enumerate(OFFSETS):
            zq = lax.rem(z + by, 4)
            for k in range(4):
                at = pl.ds(pl.multiple_of(k * 4 * rows + zq * rows, rows), rows)
                to[q, k * rows : (k + 1) * rows, :] = nat[at, :width].astype(bf16)

    sort(place_ref, 4 * rows)
    for c in copies:
        c.wait()
    nat[...] = dot(jnp.concatenate(chooses, axis=1), picked[...])
    sort(part_ref, nat.shape[1])
    wcopy.wait()


def send_body(part_ref, w_ref, *refs):
    outs, (wbuf, wsems) = refs[-8:-2], refs[-2:]
    copies = send_copies(w_ref, wbuf, wsems, outs[0].shape[1] // 2)
    send_blocks(part_ref, PAIRS[0], wbuf, copies, (outs[:1], outs[1:2]))
    send_blocks(part_ref, PAIRS[1], wbuf, None, (outs[2:4], outs[4:6]))


def more_body(pair, part_ref, w_ref, *refs):
    out_a, out_b, wbuf, wsems = refs[-4:]
    copies = send_copies(w_ref, wbuf, wsems, out_a.shape[1] // 2)
    send_blocks(part_ref, pair, wbuf, copies, ((out_a,), (out_b,)))


def mid_body(pair, pieces, part_ref, w_ref, *refs):
    out_a, out_b, wbuf, sems = refs[-4:]
    x = lax.axis_index("x")
    cols = out_a.shape[1]
    copies = [column(w_ref, partner(x, 1 - k), cols, wbuf.at[k], sems.at[k]) for k in range(2)]
    for c in copies:
        c.start()
    tile = cols // 4
    for kind, to in enumerate((out_a, out_b)):
        rows = chunk(part_ref, pair[kind])
        came = refs[kind * pieces : (kind + 1) * pieces]
        copies[kind].wait()
        for c in range(4):
            at = slice(c * tile, (c + 1) * tile)
            out = dot(rows, wbuf[kind, :, at]) + stacked(came, slice(cols + c * tile, cols + (c + 1) * tile))
            to[:, at] = out.astype(bf16)


def own_body(stage, pieces, part_ref, place_ref, w_ref, t0, t1, t2, t3, *refs):
    firsts = refs[:pieces], refs[pieces : 2 * pieces]
    seconds, refs = refs[2 * pieces : 2 * pieces + 2], refs[2 * pieces + 2 :]
    wbuf, sem = refs[-2:]
    x = lax.axis_index("x")
    cols = t0.shape[1]
    wcopy = column(w_ref, x, cols, wbuf, sem)
    wcopy.start()
    wcopy.wait()
    tile = cols // 4
    for kind, (first, second) in enumerate(zip(firsts, seconds, strict=True)):
        _, at, of = PAIRS[stage][kind]
        rows = chunk(part_ref, PAIRS[stage][kind])
        place = chunk(place_ref, PAIRS[stage][kind])
        n = rows.shape[0]
        square = jnp.zeros((n, 1), f32)
        here = slice(at * n, (at + 1) * n)
        for c in range(4):
            cs = slice(c * tile, (c + 1) * tile)
            near = slice((c % 2) * tile, (c % 2 + 1) * tile)
            table = jnp.concatenate([t[:, cs] for t in (t0, t1, t2, t3)], axis=0)
            out = dot(rows, wbuf[:, cs]) + dot(place, table)
            out += stacked(first, cs) + second[:, cs].astype(f32)
            if stage == 0:
                refs[-4 + c // 2][here, near] = out.astype(bf16)
            elif stage == 1:
                if kind == c // 2:
                    out += refs[kind][:, near].astype(f32)
                refs[-4 + kind][:, cs] = out.astype(bf16)
            else:
                out += refs[0][here, cs].astype(f32) + refs[1][here, cs].astype(f32)
                refs[-4][here, cs] = out
                square += jnp.sum(out * out, axis=1, keepdims=True)
        if stage == 2:
            refs[-3][here, :] = square


def own_half(every, half):
    g = lax.axis_index("group")
    width = every.shape[1] // 2
    return every[:, pl.ds(pl.multiple_of((g if half == 0 else 1 - g) * width, width), width)]


def map_body(every, maps, token, out):
    out[...] = dot(own_half(every, 0), maps[...])


def mapped_half(every, maps, token):
    tok, cols = every.shape[0], maps.shape[1]
    return pl.pallas_call(
        map_body,
        grid=(4,),
        out_shape=jax.ShapeDtypeStruct((tok, 4 * cols), f32),
        in_specs=[
            pl.BlockSpec(every.shape, lambda c: (0, 0)),
            pl.BlockSpec((every.shape[1] // 2, cols), lambda c: (c, 0)),
            ANY,
        ],
        out_specs=pl.BlockSpec((tok, cols), lambda c: (0, c)),
        compiler_params=pltpu.CompilerParams(vmem_limit_bytes=20 * 1024 * 1024),
        cost_estimate=pl.CostEstimate(flops=1, bytes_accessed=1, transcendentals=0),
        name="mapped",
    )(every, maps, token)


def back_body(every, mapped, pre, gain, s0, s1, s2, s3, own_map, other_map, *refs):
    outs, (flipped, whole) = refs[:4], refs[4:]
    x, g = lax.axis_index("x"), lax.axis_index("group")
    rows = outs[0].shape[0]
    cols = own_map.shape[1]
    d_half = own_map.shape[0] // 4
    total = s0[...] + s1[...] + s2[...] + s3[...]
    inverse = lax.rsqrt(total / (16 * cols) + eps)
    theirs = own_half(every, 1)
    for c in range(4):
        cs = slice(c * cols, (c + 1) * cols)
        gains = gain[pl.ds(pl.multiple_of((x * 4 + c) * cols, cols), cols)]
        aligned = (pre[:, cs] * inverse * gains[None, :]).astype(bf16)
        full = mapped[:, cs] + dot(theirs, other_map[c * d_half : (c + 1) * d_half, :])
        flipped[cs, :] = (full - aligned.astype(f32)).T.astype(bf16)
    step = d_half // 7
    for which, buf in ((1 - g, other_map), (g, own_map)):
        for j in range(7):
            got = jnp.zeros((step, 4 * rows), f32)
            for c in range(4):
                at = slice(c * d_half + j * step, c * d_half + (j + 1) * step)
                got += dot(buf[at, :], flipped[c * cols : (c + 1) * cols, :])
            to = pl.ds(pl.multiple_of(which * d_half + j * step, step), step)
            whole[:, to] = got.T.astype(bf16)
    for k, out in enumerate(outs):
        out[...] = whole[pl.ds(pl.multiple_of(lax.rem(x + k, 4) * rows, rows), rows), :]


def back_blocks(every, mapped, pre, gain, squares, own_map, other_map):
    rows, d_student = every.shape[0] // 4, every.shape[1]
    return call(
        back_body,
        [((rows, d_student), bf16)] * 4,
        [every, mapped, pre, gain, *squares, own_map, other_map],
        [VMEM] * 10,
        [pltpu.VMEM(mapped.shape[::-1], bf16), pltpu.VMEM(every.shape, bf16)],
        name="back",
        limit=32,
    )


def final_body(hidden, gain, p0, p1, p2, p3, out):
    rows = hidden[...].astype(f32)
    rstd = lax.rsqrt(jnp.mean(rows * rows, axis=1, keepdims=True) + eps)
    xhat = rows * rstd
    summed = (p0[...].astype(f32) + p1[...].astype(f32)) + (p2[...].astype(f32) + p3[...].astype(f32))
    scaled = summed * gain[...][None, :]
    out[...] = rstd * (scaled - xhat * jnp.mean(scaled * xhat, axis=1, keepdims=True))


def shards(
    contexts,
    picks,
    teacher_out,
    teacher_residual,
    teacher_gain,
    student_hidden,
    student_norm_gain,
    feature_map,
    positions,
):
    prompts, _, resp, depth = contexts.shape
    cols = teacher_out.shape[1] // 4
    rows, d_student = student_hidden.shape
    tok = 4 * rows

    own_map = lax.all_gather(feature_map, ("zh", "zl", "y"), axis=0, tiled=True)

    prepared = call(
        prep_body,
        [((rows, cols), bf16)] * 4,
        [teacher_residual],
        [VMEM],
        name="prep",
        moved=4 << 20,
    )
    table = [prepared[0]] + [shift(prepared[k], "x", k) for k in (1, 2, 3)]
    part, place, teacher_out = call(
        functools.partial(pick_body, (prompts, resp, rows)),
        [((4, tok, depth), bf16), ((4, tok, tok), bf16), (teacher_out.shape, bf16)],
        [contexts, picks, positions, teacher_out, prepared[0]],
        [HBM, SMEM, VMEM, HBM, ANY],
        [
            pltpu.VMEM((prompts * resp, depth), bf16),
            pltpu.VMEM((prompts * resp, depth), f32),
            DMA((prompts + 1,)),
        ],
        name="pick",
        limit=40,
        moved=20 << 20,
    )
    sent = call(
        send_body,
        [((tok // 2, 2 * cols), bf16)] * 6,
        [part, teacher_out, *table],
        [VMEM, ANY] + [ANY] * 4,
        [pltpu.VMEM((2, 2, depth, cols), bf16), DMA((2, 2))],
        name="send",
    )
    first = [
        [across(sent[k], k) for k in range(2)],
        [across(sent[2 + k], k // 2) for k in range(4)],
    ]

    def more(i, n, *tokens):
        outs = call(
            functools.partial(more_body, PAIRS[i]),
            [((n, 2 * cols), bf16)] * 2,
            [part, teacher_out, *tokens],
            [VMEM, ANY] + [ANY] * len(tokens),
            [pltpu.VMEM((2, 2, depth, cols), bf16), DMA((2, 2))],
            name=f"more{i}",
        )
        first.append([across(outs[k], k) for k in range(2)])
        return outs[0]

    def mid(i, *tokens):
        n = tok // PAIRS[i][0][2]
        outs = call(
            functools.partial(mid_body, PAIRS[i], len(first[i]) // 2),
            [((n, cols), bf16)] * 2,
            [part, teacher_out, *first[i], *tokens],
            [VMEM, ANY] + [VMEM] * len(first[i]) + [ANY] * len(tokens),
            [pltpu.VMEM((2, depth, cols), bf16), DMA((2,))],
            name=f"mid{i}",
        )
        return outs[0], [across(outs[k], 1 - k) for k in range(2)]

    def own(i, second, extra, outs, *tokens):
        return call(
            functools.partial(own_body, i, len(first[i]) // 2),
            outs,
            [part, place, teacher_out, *table, *first[i], *second, *extra, *tokens],
            [VMEM, VMEM, ANY] + [VMEM] * (6 + len(first[i]) + len(extra)) + [ANY] * len(tokens),
            [pltpu.VMEM((depth, cols), bf16), DMA],
            name=f"own{i}",
        )

    t, second0 = mid(0)
    t, second1 = mid(1, t)
    far = own(0, second0, (), [((tok, cols // 2), bf16)] * 2, t)
    far_z = shift(far[0], "zh", 1), shift(far[1], "zh", -1)

    normed = call(
        norm_body, [((rows, d_student), bf16)], [student_hidden, student_norm_gain, far[0]], [VMEM, VMEM, ANY], name="norm"
    )[0]
    two = call(
        functools.partial(merge_body, lambda x: lax.rem(x, 2)),
        [((2 * rows, d_student), bf16)],
        [normed, across(normed, 0)],
        [VMEM] * 2,
        name="two",
    )[0]
    near = own(1, second1, far_z, [((tok, cols), bf16)] * 2, two)
    near_z = shift(near[0], "zh", 1), shift(near[1], "zh", -1)
    t = more(2, tok // 2, near[0])
    t, second2 = mid(2, t)
    every = call(
        functools.partial(merge_body, lambda x: x // 2),
        [((tok, d_student), bf16)],
        [two, across(two, 1), t],
        [VMEM] * 2 + [ANY],
        name="every",
    )[0]
    pre, square = own(2, second2, near_z, [((tok, cols), f32), ((tok, 1), f32)], every)
    own_map = gate(own_map, square)
    other_map = lax.ppermute(own_map, "group", [(0, 1), (1, 0)])
    squares = [square] + [shift(square, "x", k) for k in (1, 2, 3)]
    mapped = mapped_half(every, own_map, square)
    backs = back_blocks(every, mapped, pre, teacher_gain, squares, own_map, other_map)
    parts = [backs[0]] + [shift(backs[k], "x", k) for k in (1, 2, 3)]
    return call(
        final_body,
        [((rows, d_student), f32)],
        [student_hidden, student_norm_gain, *parts],
        [VMEM] * 6,
        name="final",
    )[0]


def solution(mesh):
    axes = ("group", "zl", "y", "x", "zh")
    fine = Mesh(mesh.devices.reshape(2, 2, 4, 4, 4), axes)
    gd, mp = ("group", "zl", "y"), ("x", "zh")
    in_specs = (
        P(gd, None, None, mp),
        P(gd),
        P(mp, None),
        P(axes, None),
        P(),
        P(axes, None),
        P(),
        P(gd, mp),
        P(gd, None),
    )
    return jax.shard_map(
        shards, mesh=fine, in_specs=in_specs, out_specs=P(axes, None), check_vma=False
    )
```

```python
import functools
import jax
import jax.numpy as jnp
from jax import lax
from jax.experimental import pallas as pl
from jax.experimental.pallas import tpu as pltpu
from jax.sharding import Mesh, PartitionSpec as P

eps = 1e-06
f32, bf16 = jnp.float32, jnp.bfloat16
VMEM = pl.BlockSpec(memory_space=pltpu.VMEM)
SMEM = pl.BlockSpec(memory_space=pltpu.SMEM)
ANY = pl.BlockSpec(memory_space=pl.ANY)
HBM = pl.BlockSpec(memory_space=pltpu.HBM)
DMA = pltpu.SemaphoreType.DMA
OFFSETS = (2, 1, 3, 0)
PAD = 512
PAIRS = (((0, 0, 2), (0, 1, 2)), ((1, 0, 1), (2, 0, 1)), ((3, 0, 2), (3, 1, 2)))


def shift(a, axis, by):
    return lax.ppermute(a, axis, [(i, (i + by) % 4) for i in range(4)])


def across(a, kind):
    return lax.ppermute(a, "x", [(i, 3 - i if kind else i ^ 1) for i in range(4)])


def partner(x, kind):
    return 3 - x if kind else x + 1 - 2 * lax.rem(x, 2)


def dot(a, b):
    return jnp.dot(a, b, preferred_element_type=f32)


def call(body, outs, ins, specs, scratch=(), name=None, aliases=None, out_spec=VMEM, limit=20, moved=1):
    return pl.pallas_call(
        body,
        out_shape=[jax.ShapeDtypeStruct(s, t) for s, t in outs],
        in_specs=specs,
        out_specs=[out_spec] * len(outs),
        scratch_shapes=list(scratch),
        compiler_params=pltpu.CompilerParams(vmem_limit_bytes=limit * 1024 * 1024),
        cost_estimate=pl.CostEstimate(flops=1, bytes_accessed=moved, transcendentals=0),
        input_output_aliases=aliases or {},
        name=name,
    )(*ins)


def gate(a, *tokens):
    return call(
        lambda *refs: None,
        [(a.shape, a.dtype)],
        [a, *tokens],
        [ANY] * (1 + len(tokens)),
        name="gate",
        aliases={0: 0},
        out_spec=ANY,
    )[0]


def column(w_ref, index, cols, buf, sem):
    start = pl.multiple_of(index * cols, cols)
    return pltpu.make_async_copy(w_ref.at[:, pl.ds(start, cols)], buf, sem)


def chunk(part_ref, where):
    q, at, of = where
    n = part_ref.shape[1] // of
    return part_ref[q, at * n : (at + 1) * n, :]


def prep_body(residual, *outs):
    x = lax.axis_index("x")
    cols = residual.shape[1] // 4
    for k, out in enumerate(outs):
        start = pl.multiple_of(lax.rem(x + k, 4) * cols, cols)
        out[...] = residual[:, pl.ds(start, cols)]


def norm_body(hidden, gain, token, out):
    rows = hidden[...].astype(f32)
    rstd = lax.rsqrt(jnp.mean(rows * rows, axis=1, keepdims=True) + eps)
    out[...] = (rows * rstd * gain[...][None, :]).astype(bf16)


def two_body(mine, came, *refs):
    out = refs[-1]
    n = mine.shape[0]
    low = lax.rem(lax.axis_index("x"), 2)
    out[pl.ds(pl.multiple_of(low * n, n), n), :] = mine[...]
    out[pl.ds(pl.multiple_of((1 - low) * n, n), n), :] = came[...]


def every_body(run, mine, came, token, out, wide):
    n = mine.shape[0]
    pad = out.shape[1] // 8
    low = lax.axis_index("x") // 2
    wide[...] = jnp.zeros_like(wide)
    for src, at in ((mine, low), (came, 1 - low)):
        here = pl.ds(pl.multiple_of(at * n, n), n)
        rows = src[...].astype(f32)
        for core in range(2):
            for y in range(4):
                for zl in range(2):
                    first = ((core * 2 + zl) * 4 + y) * run
                    to = (core * 4 + y) * pad + zl * run
                    wide[here, to : to + run] = rows[:, first : first + run]
    out[...] = wide[...].astype(bf16)


def send_blocks(part_ref, pair, wbuf, copies, outs):
    cols = wbuf.shape[-1]
    tile = cols // 4
    for kind in range(2):
        rows = chunk(part_ref, pair[kind])
        n = outs[kind][0].shape[0]
        for h in range(2):
            if copies:
                copies[kind][h].wait()
            for c in range(4):
                out = dot(rows, wbuf[kind, h, :, c * tile : (c + 1) * tile]).astype(bf16)
                for i, to in enumerate(outs[kind]):
                    to[:, h * cols + c * tile : h * cols + (c + 1) * tile] = out[i * n : (i + 1) * n]


def stacked(pieces, cs):
    return jnp.concatenate([r[:, cs].astype(f32) for r in pieces], axis=0)


def send_copies(w_ref, wbuf, sems, cols):
    x = lax.axis_index("x")
    copies = []
    for kind in range(2):
        p = partner(x, kind)
        copies.append(
            [column(w_ref, b, cols, wbuf.at[kind, h], sems.at[kind, h]) for h, b in enumerate((p, partner(p, 1 - kind)))]
        )
        for c in copies[-1]:
            c.start()
    return copies


def pick_body(sizes, ctx_ref, picks_ref, pos_ref, w_ref, token, part_ref, place_ref, w_out, picked, nat, sems):
    prompts, resp, rows = sizes
    x, z = lax.axis_index("x"), lax.axis_index("zh")
    tokens = prompts * resp
    copies = []
    for p in range(prompts):
        copies.append(
            pltpu.make_async_copy(
                ctx_ref.at[p, picks_ref[p]], picked.at[pl.ds(p * resp, resp), :], sems.at[p]
            )
        )
        copies[-1].start()
    wcopy = pltpu.make_async_copy(w_ref, w_out, sems.at[prompts])
    wcopy.start()
    lanes = min(128, tokens)
    want = jnp.broadcast_to(pos_ref[...], (lanes, tokens)).T
    lane = lax.broadcasted_iota(jnp.int32, (tokens, lanes), 1)
    chooses = [(want == lane + c * lanes).astype(bf16) for c in range(tokens // lanes)]
    slot = lax.broadcasted_iota(jnp.int32, (tokens, 4 * rows), 1)
    row = (lax.rem(x - slot // rows + 4, 4) * 4 + z) * rows + lax.rem(slot, rows)
    nat[:, : 4 * rows] = (want[:, : 4 * rows] == row).astype(f32)

    def sort(to, width):
        for q, by in enumerate(OFFSETS):
            zq = lax.rem(z + by, 4)
            for k in range(4):
                at = pl.ds(pl.multiple_of(k * 4 * rows + zq * rows, rows), rows)
                to[q, k * rows : (k + 1) * rows, :] = nat[at, :width].astype(bf16)

    sort(place_ref, 4 * rows)
    for c in copies:
        c.wait()
    nat[...] = dot(jnp.concatenate(chooses, axis=1), picked[...])
    sort(part_ref, nat.shape[1])
    wcopy.wait()


def send_body(part_ref, w_ref, *refs):
    outs, (wbuf, wsems) = refs[-8:-2], refs[-2:]
    copies = send_copies(w_ref, wbuf, wsems, outs[0].shape[1] // 2)
    send_blocks(part_ref, PAIRS[0], wbuf, copies, (outs[:1], outs[1:2]))
    send_blocks(part_ref, PAIRS[1], wbuf, None, (outs[2:4], outs[4:6]))


def more_body(pair, part_ref, w_ref, *refs):
    out_a, out_b, wbuf, wsems = refs[-4:]
    copies = send_copies(w_ref, wbuf, wsems, out_a.shape[1] // 2)
    send_blocks(part_ref, pair, wbuf, copies, ((out_a,), (out_b,)))


def mid_body(pair, pieces, part_ref, w_ref, *refs):
    out_a, out_b, wbuf, sems = refs[-4:]
    x = lax.axis_index("x")
    cols = out_a.shape[1]
    copies = [column(w_ref, partner(x, 1 - k), cols, wbuf.at[k], sems.at[k]) for k in range(2)]
    for c in copies:
        c.start()
    tile = cols // 4
    for kind, to in enumerate((out_a, out_b)):
        rows = chunk(part_ref, pair[kind])
        came = refs[kind * pieces : (kind + 1) * pieces]
        copies[kind].wait()
        for c in range(4):
            at = slice(c * tile, (c + 1) * tile)
            out = dot(rows, wbuf[kind, :, at]) + stacked(came, slice(cols + c * tile, cols + (c + 1) * tile))
            to[:, at] = out.astype(bf16)


def own_body(stage, pieces, part_ref, place_ref, w_ref, t0, t1, t2, t3, *refs):
    firsts = refs[:pieces], refs[pieces : 2 * pieces]
    seconds, refs = refs[2 * pieces : 2 * pieces + 2], refs[2 * pieces + 2 :]
    wbuf, sem = refs[-2:]
    x = lax.axis_index("x")
    cols = t0.shape[1]
    wcopy = column(w_ref, x, cols, wbuf, sem)
    wcopy.start()
    wcopy.wait()
    tile = cols // 4
    for kind, (first, second) in enumerate(zip(firsts, seconds, strict=True)):
        _, at, of = PAIRS[stage][kind]
        rows = chunk(part_ref, PAIRS[stage][kind])
        place = chunk(place_ref, PAIRS[stage][kind])
        n = rows.shape[0]
        square = jnp.zeros((n, 1), f32)
        here = slice(at * n, (at + 1) * n)
        for c in range(4):
            cs = slice(c * tile, (c + 1) * tile)
            near = slice((c % 2) * tile, (c % 2 + 1) * tile)
            table = jnp.concatenate([t[:, cs] for t in (t0, t1, t2, t3)], axis=0)
            out = dot(rows, wbuf[:, cs]) + dot(place, table)
            out += stacked(first, cs) + second[:, cs].astype(f32)
            if stage == 0:
                refs[-4 + c // 2][here, near] = out.astype(bf16)
            elif stage == 1:
                if kind == c // 2:
                    out += refs[kind][:, near].astype(f32)
                refs[-4 + kind][:, cs] = out.astype(bf16)
            else:
                out += refs[0][here, cs].astype(f32) + refs[1][here, cs].astype(f32)
                refs[-4][here, cs] = out
                square += jnp.sum(out * out, axis=1, keepdims=True)
        if stage == 2:
            refs[-3][here, :] = square


def half_start(every, half):
    g = lax.axis_index("group")
    width = every.shape[1] // 2
    return pl.multiple_of((g if half == 0 else 1 - g) * width, width)


def map_rows(every, start, maps, c):
    pad, run = every.shape[1] // 8, maps.shape[2]
    got = 0.0
    for y in range(4):
        rows = every[:, pl.ds(pl.multiple_of(start + y * pad, pad), pad)][:, :run]
        got += dot(rows, maps[y, c])
    return got


def map_body(every, maps, token, out):
    out[...] = map_rows(every, half_start(every, 0), maps, 0)


def mapped_half(every, maps, token):
    tok, cols = every.shape[0], maps.shape[3]
    return pl.pallas_call(
        map_body,
        grid=(4,),
        out_shape=jax.ShapeDtypeStruct((tok, 4 * cols), f32),
        in_specs=[
            pl.BlockSpec(every.shape, lambda c: (0, 0)),
            pl.BlockSpec((4, 1, *maps.shape[2:]), lambda c: (0, c, 0, 0)),
            ANY,
        ],
        out_specs=pl.BlockSpec((tok, cols), lambda c: (0, c)),
        compiler_params=pltpu.CompilerParams(vmem_limit_bytes=20 * 1024 * 1024),
        cost_estimate=pl.CostEstimate(flops=1, bytes_accessed=1, transcendentals=0),
        name="mapped",
    )(every, maps, token)


def back_body(every, mapped, pre, gain, s0, s1, s2, s3, own, other, o0, o1, o2, o3, flipped, whole):
    x, g = lax.axis_index("x"), lax.axis_index("group")
    cols, run = own.shape[3], own.shape[2] // 2
    total = s0[...] + s1[...] + s2[...] + s3[...]
    inverse = lax.rsqrt(total / (16 * cols) + eps)
    start = half_start(every, 1)
    for c in range(4):
        cs = slice(c * cols, (c + 1) * cols)
        gains = gain[pl.ds(pl.multiple_of((x * 4 + c) * cols, cols), cols)]
        aligned = (pre[:, cs] * inverse * gains[None, :]).astype(bf16)
        full = mapped[:, cs] + map_rows(every, start, other, c)
        flipped[cs, :] = (full - aligned.astype(f32)).T.astype(bf16)
    for i, maps in enumerate((other, own)):
        for y in range(4):
            got = 0.0
            for c in range(4):
                got += dot(maps[y, c], flipped[c * cols : (c + 1) * cols, :])
            got = got.T
            for zl in range(2):
                to = (zl * 4 + y) * run
                whole[i, :, to : to + run] = got[:, zl * run : (zl + 1) * run]
    rows, width = o0.shape[0], whole.shape[2]
    for k, out in enumerate((o0, o1, o2, o3)):
        at = pl.ds(pl.multiple_of(lax.rem(x + k, 4) * rows, rows), rows)
        for i, core in enumerate((1 - g, g)):
            out[:, pl.ds(pl.multiple_of(core * width, width), width)] = whole[i, at, :].astype(bf16)


def final_body(hidden, gain, p0, p1, p2, p3, out):
    rows = hidden[...].astype(f32)
    rstd = lax.rsqrt(jnp.mean(rows * rows, axis=1, keepdims=True) + eps)
    xhat = rows * rstd
    summed = (p0[...].astype(f32) + p1[...].astype(f32)) + (p2[...].astype(f32) + p3[...].astype(f32))
    scaled = summed * gain[...][None, :]
    out[...] = rstd * (scaled - xhat * jnp.mean(scaled * xhat, axis=1, keepdims=True))


def shards(
    contexts,
    picks,
    teacher_out,
    teacher_residual,
    teacher_gain,
    student_hidden,
    student_norm_gain,
    feature_map,
    positions,
):
    prompts, _, resp, depth = contexts.shape
    cols = teacher_out.shape[1] // 4
    rows, d_student = student_hidden.shape
    tok = 4 * rows
    d_wide = 8 * PAD

    along_z = lax.all_gather(feature_map, ("zh", "zl"), axis=0, tiled=True)

    prepared = call(
        prep_body,
        [((rows, cols), bf16)] * 4,
        [teacher_residual],
        [VMEM],
        name="prep",
        moved=4 << 20,
    )
    table = [prepared[0]] + [shift(prepared[k], "x", k) for k in (1, 2, 3)]
    part, place, teacher_out = call(
        functools.partial(pick_body, (prompts, resp, rows)),
        [((4, tok, depth), bf16), ((4, tok, tok), bf16), (teacher_out.shape, bf16)],
        [contexts, picks, positions, teacher_out, prepared[0]],
        [HBM, SMEM, VMEM, HBM, ANY],
        [
            pltpu.VMEM((prompts * resp, depth), bf16),
            pltpu.VMEM((prompts * resp, depth), f32),
            DMA((prompts + 1,)),
        ],
        name="pick",
        limit=40,
        moved=20 << 20,
    )
    sent = call(
        send_body,
        [((tok // 2, 2 * cols), bf16)] * 6,
        [part, teacher_out, *table],
        [VMEM, ANY] + [ANY] * 4,
        [pltpu.VMEM((2, 2, depth, cols), bf16), DMA((2, 2))],
        name="send",
    )
    first = [
        [across(sent[k], k) for k in range(2)],
        [across(sent[2 + k], k // 2) for k in range(4)],
    ]

    last = call(
        functools.partial(more_body, PAIRS[2]),
        [((tok // 2, 2 * cols), bf16)] * 2,
        [part, teacher_out, sent[0]],
        [VMEM, ANY, ANY],
        [pltpu.VMEM((2, 2, depth, cols), bf16), DMA((2, 2))],
        name="more",
    )

    def mid(i, *tokens):
        n = tok // PAIRS[i][0][2]
        outs = call(
            functools.partial(mid_body, PAIRS[i], len(first[i]) // 2),
            [((n, cols), bf16)] * 2,
            [part, teacher_out, *first[i], *tokens],
            [VMEM, ANY] + [VMEM] * len(first[i]) + [ANY] * len(tokens),
            [pltpu.VMEM((2, depth, cols), bf16), DMA((2,))],
            name=f"mid{i}",
        )
        return outs[0], [across(outs[k], 1 - k) for k in range(2)]

    def own(i, second, extra, outs, *tokens):
        return call(
            functools.partial(own_body, i, len(first[i]) // 2),
            outs,
            [part, place, teacher_out, *table, *first[i], *second, *extra, *tokens],
            [VMEM, VMEM, ANY] + [VMEM] * (6 + len(first[i]) + len(extra)) + [ANY] * len(tokens),
            [pltpu.VMEM((depth, cols), bf16), DMA],
            name=f"own{i}",
        )

    t, second0 = mid(0, last[0])
    along_z = gate(along_z, t, first[1][0], first[1][2])
    own_map = lax.all_gather(along_z, "y", axis=0, tiled=True).reshape(4, 4, -1, along_z.shape[1])
    t, second1 = mid(1, t)
    far = own(0, second0, (), [((tok, cols // 2), bf16)] * 2, t)
    far_z = shift(far[0], "zh", 1), shift(far[1], "zh", -1)

    normed = call(
        norm_body, [((rows, d_student), bf16)], [student_hidden, student_norm_gain, far[0]], [VMEM, VMEM, ANY], name="norm"
    )[0]
    two = call(
        two_body, [((2 * rows, d_student), bf16)], [normed, across(normed, 0)], [VMEM, VMEM], name="two"
    )[0]
    near = own(1, second1, far_z, [((tok, cols), bf16)] * 2, two)
    near_z = shift(near[0], "zh", 1), shift(near[1], "zh", -1)
    last = call(
        lambda *refs: None,
        [((tok // 2, 2 * cols), bf16)] * 2,
        [*last, near[0]],
        [VMEM, VMEM, ANY],
        name="release",
        aliases={0: 0, 1: 1},
    )
    first.append([across(last[k], k) for k in range(2)])
    t, second2 = mid(2, near[0])
    every = call(
        functools.partial(every_body, feature_map.shape[0]),
        [((tok, d_wide), bf16)],
        [two, across(two, 1), t],
        [VMEM, VMEM, ANY],
        [pltpu.VMEM((tok, d_wide), f32)],
        name="every",
    )[0]
    pre, square = own(2, second2, near_z, [((tok, cols), f32), ((tok, 1), f32)], every)
    own_map = gate(own_map, square)
    other_map = lax.ppermute(own_map, "group", [(0, 1), (1, 0)])
    squares = [square] + [shift(square, "x", k) for k in (1, 2, 3)]
    mapped = mapped_half(every, own_map, square)
    backs = call(
        back_body,
        [((rows, d_student), bf16)] * 4,
        [every, mapped, pre, teacher_gain, *squares, own_map, other_map],
        [VMEM] * 10,
        [pltpu.VMEM((4 * own_map.shape[3], tok), bf16), pltpu.VMEM((2, tok, d_student // 2), f32)],
        name="back",
        limit=32,
    )
    parts = [backs[0]] + [shift(backs[k], "x", k) for k in (1, 2, 3)]
    return call(
        final_body,
        [((rows, d_student), f32)],
        [student_hidden, student_norm_gain, *parts],
        [VMEM] * 6,
        name="final",
    )[0]


def solution(mesh):
    axes = ("group", "zl", "y", "x", "zh")
    fine = Mesh(mesh.devices.reshape(2, 2, 4, 4, 4), axes)
    gd, mp = ("group", "zl", "y"), ("x", "zh")
    in_specs = (
        P(gd, None, None, mp),
        P(gd),
        P(mp, None),
        P(axes, None),
        P(),
        P(axes, None),
        P(),
        P(gd, mp),
        P(gd, None),
    )
    return jax.shard_map(
        shards, mesh=fine, in_specs=in_specs, out_specs=P(axes, None), check_vma=False
    )
```

```python
import functools
import jax
import jax.numpy as jnp
from jax import lax
from jax.experimental import pallas as pl
from jax.experimental.pallas import tpu as pltpu
from jax.sharding import Mesh, PartitionSpec as P

eps = 1e-06
f32, bf16 = jnp.float32, jnp.bfloat16
VMEM = pl.BlockSpec(memory_space=pltpu.VMEM)
SMEM = pl.BlockSpec(memory_space=pltpu.SMEM)
ANY = pl.BlockSpec(memory_space=pl.ANY)
HBM = pl.BlockSpec(memory_space=pltpu.HBM)
DMA = pltpu.SemaphoreType.DMA
OFFSETS = (2, 1, 3, 0)
PAD = 512
PAIRS = (((0, 0, 2), (0, 1, 2)), ((1, 0, 1), (2, 0, 1)), ((3, 0, 2), (3, 1, 2)))


def shift(a, axis, by):
    return lax.ppermute(a, axis, [(i, (i + by) % 4) for i in range(4)])


def across(a, kind):
    return lax.ppermute(a, "x", [(i, 3 - i if kind else i ^ 1) for i in range(4)])


def partner(x, kind):
    return 3 - x if kind else x + 1 - 2 * lax.rem(x, 2)


def dot(a, b):
    return jnp.dot(a, b, preferred_element_type=f32)


def call(body, outs, ins, specs, scratch=(), name=None, aliases=None, out_spec=VMEM, limit=20, moved=1):
    return pl.pallas_call(
        body,
        out_shape=[jax.ShapeDtypeStruct(s, t) for s, t in outs],
        in_specs=specs,
        out_specs=[out_spec] * len(outs),
        scratch_shapes=list(scratch),
        compiler_params=pltpu.CompilerParams(vmem_limit_bytes=limit * 1024 * 1024),
        cost_estimate=pl.CostEstimate(flops=1, bytes_accessed=moved, transcendentals=0),
        input_output_aliases=aliases or {},
        name=name,
    )(*ins)


def gate(a, *tokens):
    return call(
        lambda *refs: None,
        [(a.shape, a.dtype)],
        [a, *tokens],
        [ANY] * (1 + len(tokens)),
        name="gate",
        aliases={0: 0},
        out_spec=ANY,
    )[0]


def column(w_ref, index, cols, buf, sem):
    start = pl.multiple_of(index * cols, cols)
    return pltpu.make_async_copy(w_ref.at[:, pl.ds(start, cols)], buf, sem)


def chunk(part_ref, where):
    q, at, of = where
    n = part_ref.shape[1] // of
    return part_ref[q, at * n : (at + 1) * n, :]


def prep_body(residual, *outs):
    x = lax.axis_index("x")
    cols = residual.shape[1] // 4
    for k, out in enumerate(outs):
        start = pl.multiple_of(lax.rem(x + k, 4) * cols, cols)
        out[...] = residual[:, pl.ds(start, cols)]


def norm_body(hidden, gain, token, out):
    rows = hidden[...].astype(f32)
    rstd = lax.rsqrt(jnp.mean(rows * rows, axis=1, keepdims=True) + eps)
    out[...] = (rows * rstd * gain[...][None, :]).astype(bf16)


def two_body(mine, came, *refs):
    out = refs[-1]
    n = mine.shape[0]
    low = lax.rem(lax.axis_index("x"), 2)
    out[pl.ds(pl.multiple_of(low * n, n), n), :] = mine[...]
    out[pl.ds(pl.multiple_of((1 - low) * n, n), n), :] = came[...]


def every_body(run, mine, came, token, out, wide):
    n = mine.shape[0]
    pad = out.shape[1] // 8
    low = lax.axis_index("x") // 2
    wide[...] = jnp.zeros_like(wide)
    for src, at in ((mine, low), (came, 1 - low)):
        here = pl.ds(pl.multiple_of(at * n, n), n)
        rows = src[...].astype(f32)
        for core in range(2):
            for y in range(4):
                for zl in range(2):
                    first = ((core * 2 + zl) * 4 + y) * run
                    to = (core * 4 + y) * pad + zl * run
                    wide[here, to : to + run] = rows[:, first : first + run]
    out[...] = wide[...].astype(bf16)


def send_blocks(part_ref, pair, wbuf, copies, outs):
    cols = wbuf.shape[-1]
    tile = cols // 4
    for kind in range(2):
        rows = chunk(part_ref, pair[kind])
        n = outs[kind][0].shape[0]
        for h in range(2):
            if copies:
                copies[kind][h].wait()
            for c in range(4):
                out = dot(rows, wbuf[kind, h, :, c * tile : (c + 1) * tile]).astype(bf16)
                for i, to in enumerate(outs[kind]):
                    to[:, h * cols + c * tile : h * cols + (c + 1) * tile] = out[i * n : (i + 1) * n]


def stacked(pieces, cs):
    return jnp.concatenate([r[:, cs].astype(f32) for r in pieces], axis=0)


def send_copies(w_ref, wbuf, sems, cols):
    x = lax.axis_index("x")
    copies = []
    for kind in range(2):
        p = partner(x, kind)
        copies.append(
            [column(w_ref, b, cols, wbuf.at[kind, h], sems.at[kind, h]) for h, b in enumerate((p, partner(p, 1 - kind)))]
        )
        for c in copies[-1]:
            c.start()
    return copies


def pick_body(sizes, ctx_ref, picks_ref, pos_ref, w_ref, token, part_ref, place_ref, w_out, picked, nat, sems):
    prompts, resp, rows = sizes
    x, z = lax.axis_index("x"), lax.axis_index("zh")
    tokens = prompts * resp
    copies = []
    for p in range(prompts):
        copies.append(
            pltpu.make_async_copy(
                ctx_ref.at[p, picks_ref[p]], picked.at[pl.ds(p * resp, resp), :], sems.at[p]
            )
        )
        copies[-1].start()
    wcopy = pltpu.make_async_copy(w_ref, w_out, sems.at[prompts])
    wcopy.start()
    lanes = min(128, tokens)
    want = jnp.broadcast_to(pos_ref[...], (lanes, tokens)).T
    lane = lax.broadcasted_iota(jnp.int32, (tokens, lanes), 1)
    chooses = [(want == lane + c * lanes).astype(bf16) for c in range(tokens // lanes)]
    slot = lax.broadcasted_iota(jnp.int32, (tokens, 4 * rows), 1)
    row = (lax.rem(x - slot // rows + 4, 4) * 4 + z) * rows + lax.rem(slot, rows)
    nat[:, : 4 * rows] = (want[:, : 4 * rows] == row).astype(f32)

    def sort(to, width):
        for q, by in enumerate(OFFSETS):
            zq = lax.rem(z + by, 4)
            for k in range(4):
                at = pl.ds(pl.multiple_of(k * 4 * rows + zq * rows, rows), rows)
                to[q, k * rows : (k + 1) * rows, :] = nat[at, :width].astype(bf16)

    sort(place_ref, 4 * rows)
    for c in copies:
        c.wait()
    nat[...] = dot(jnp.concatenate(chooses, axis=1), picked[...])
    sort(part_ref, nat.shape[1])
    wcopy.wait()


def send_body(part_ref, w_ref, *refs):
    outs, (wbuf, wsems) = refs[-8:-2], refs[-2:]
    copies = send_copies(w_ref, wbuf, wsems, outs[0].shape[1] // 2)
    send_blocks(part_ref, PAIRS[0], wbuf, copies, (outs[:1], outs[1:2]))
    send_blocks(part_ref, PAIRS[1], wbuf, None, (outs[2:4], outs[4:6]))


def more_body(pair, part_ref, w_ref, *refs):
    out_a, out_b, wbuf, wsems = refs[-4:]
    copies = send_copies(w_ref, wbuf, wsems, out_a.shape[1] // 2)
    send_blocks(part_ref, pair, wbuf, copies, ((out_a,), (out_b,)))


def mid_body(pair, pieces, part_ref, w_ref, *refs):
    out_a, out_b, wbuf, sems = refs[-4:]
    x = lax.axis_index("x")
    cols = out_a.shape[1]
    copies = [column(w_ref, partner(x, 1 - k), cols, wbuf.at[k], sems.at[k]) for k in range(2)]
    for c in copies:
        c.start()
    tile = cols // 4
    for kind, to in enumerate((out_a, out_b)):
        rows = chunk(part_ref, pair[kind])
        came = refs[kind * pieces : (kind + 1) * pieces]
        copies[kind].wait()
        for c in range(4):
            at = slice(c * tile, (c + 1) * tile)
            out = dot(rows, wbuf[kind, :, at]) + stacked(came, slice(cols + c * tile, cols + (c + 1) * tile))
            to[:, at] = out.astype(bf16)


def own_body(stage, pieces, part_ref, place_ref, w_ref, t0, t1, t2, t3, *refs):
    firsts = refs[:pieces], refs[pieces : 2 * pieces]
    seconds, refs = refs[2 * pieces : 2 * pieces + 2], refs[2 * pieces + 2 :]
    wbuf, sem = refs[-2:]
    x = lax.axis_index("x")
    cols = t0.shape[1]
    wcopy = column(w_ref, x, cols, wbuf, sem)
    wcopy.start()
    wcopy.wait()
    tile = cols // 4
    for kind, (first, second) in enumerate(zip(firsts, seconds, strict=True)):
        _, at, of = PAIRS[stage][kind]
        rows = chunk(part_ref, PAIRS[stage][kind])
        place = chunk(place_ref, PAIRS[stage][kind])
        n = rows.shape[0]
        square = jnp.zeros((n, 1), f32)
        here = slice(at * n, (at + 1) * n)
        for c in range(4):
            cs = slice(c * tile, (c + 1) * tile)
            near = slice((c % 2) * tile, (c % 2 + 1) * tile)
            table = jnp.concatenate([t[:, cs] for t in (t0, t1, t2, t3)], axis=0)
            out = dot(rows, wbuf[:, cs]) + dot(place, table)
            out += stacked(first, cs) + second[:, cs].astype(f32)
            if stage == 0:
                refs[-4 + c // 2][here, near] = out.astype(bf16)
            elif stage == 1:
                if kind == c // 2:
                    out += refs[kind][:, near].astype(f32)
                refs[-4 + kind][:, cs] = out.astype(bf16)
            else:
                out += refs[0][here, cs].astype(f32) + refs[1][here, cs].astype(f32)
                refs[-4][here, cs] = out
                square += jnp.sum(out * out, axis=1, keepdims=True)
        if stage == 2:
            refs[-3][here, :] = square


def half_start(every, half):
    g = lax.axis_index("group")
    width = every.shape[1] // 2
    return pl.multiple_of((g if half == 0 else 1 - g) * width, width)


def map_rows(every, start, maps, c):
    pad, run = every.shape[1] // 8, maps.shape[2]
    got = 0.0
    for y in range(4):
        rows = every[:, pl.ds(pl.multiple_of(start + y * pad, pad), pad)][:, :run]
        got += dot(rows, maps[y, c])
    return got


def map_body(every, maps, token, out):
    out[...] = map_rows(every, half_start(every, 0), maps, 0)


def mapped_half(every, maps, token):
    tok, cols = every.shape[0], maps.shape[3]
    return pl.pallas_call(
        map_body,
        grid=(4,),
        out_shape=jax.ShapeDtypeStruct((tok, 4 * cols), f32),
        in_specs=[
            pl.BlockSpec(every.shape, lambda c: (0, 0)),
            pl.BlockSpec((4, 1, *maps.shape[2:]), lambda c: (0, c, 0, 0)),
            ANY,
        ],
        out_specs=pl.BlockSpec((tok, cols), lambda c: (0, c)),
        compiler_params=pltpu.CompilerParams(vmem_limit_bytes=20 * 1024 * 1024),
        cost_estimate=pl.CostEstimate(flops=1, bytes_accessed=1, transcendentals=0),
        name="mapped",
    )(every, maps, token)


def back_body(every, mapped, pre, gain, s0, s1, s2, s3, own_ref, other, o0, o1, o2, o3, flipped, whole, own, sem):
    x, g = lax.axis_index("x"), lax.axis_index("group")
    fetch = pltpu.make_async_copy(own_ref, own, sem)
    fetch.start()
    cols, run = own.shape[3], own.shape[2] // 2
    total = s0[...] + s1[...] + s2[...] + s3[...]
    inverse = lax.rsqrt(total / (16 * cols) + eps)
    start = half_start(every, 1)
    for c in range(4):
        cs = slice(c * cols, (c + 1) * cols)
        gains = gain[pl.ds(pl.multiple_of((x * 4 + c) * cols, cols), cols)]
        aligned = (pre[:, cs] * inverse * gains[None, :]).astype(bf16)
        full = mapped[:, cs] + map_rows(every, start, other, c)
        flipped[cs, :] = (full - aligned.astype(f32)).T.astype(bf16)
    for i, maps in enumerate((other, own)):
        if i == 1:
            fetch.wait()
        for y in range(4):
            got = 0.0
            for c in range(4):
                got += dot(maps[y, c], flipped[c * cols : (c + 1) * cols, :])
            got = got.T
            for zl in range(2):
                to = (zl * 4 + y) * run
                whole[i, :, to : to + run] = got[:, zl * run : (zl + 1) * run]
    rows, width = o0.shape[0], whole.shape[2]
    for k, out in enumerate((o0, o1, o2, o3)):
        at = pl.ds(pl.multiple_of(lax.rem(x + k, 4) * rows, rows), rows)
        for i, core in enumerate((1 - g, g)):
            out[:, pl.ds(pl.multiple_of(core * width, width), width)] = whole[i, at, :].astype(bf16)


def final_body(hidden, gain, p0, p1, p2, p3, out):
    rows = hidden[...].astype(f32)
    rstd = lax.rsqrt(jnp.mean(rows * rows, axis=1, keepdims=True) + eps)
    xhat = rows * rstd
    summed = (p0[...].astype(f32) + p1[...].astype(f32)) + (p2[...].astype(f32) + p3[...].astype(f32))
    scaled = summed * gain[...][None, :]
    out[...] = rstd * (scaled - xhat * jnp.mean(scaled * xhat, axis=1, keepdims=True))


def shards(
    contexts,
    picks,
    teacher_out,
    teacher_residual,
    teacher_gain,
    student_hidden,
    student_norm_gain,
    feature_map,
    positions,
):
    prompts, _, resp, depth = contexts.shape
    cols = teacher_out.shape[1] // 4
    rows, d_student = student_hidden.shape
    tok = 4 * rows
    d_wide = 8 * PAD

    along_z = lax.all_gather(feature_map, ("zh", "zl"), axis=0, tiled=True)

    prepared = call(
        prep_body,
        [((rows, cols), bf16)] * 4,
        [teacher_residual],
        [VMEM],
        name="prep",
        moved=4 << 20,
    )
    table = [prepared[0]] + [shift(prepared[k], "x", k) for k in (1, 2, 3)]
    part, place, teacher_out = call(
        functools.partial(pick_body, (prompts, resp, rows)),
        [((4, tok, depth), bf16), ((4, tok, tok), bf16), (teacher_out.shape, bf16)],
        [contexts, picks, positions, teacher_out, prepared[0]],
        [HBM, SMEM, VMEM, HBM, ANY],
        [
            pltpu.VMEM((prompts * resp, depth), bf16),
            pltpu.VMEM((prompts * resp, depth), f32),
            DMA((prompts + 1,)),
        ],
        name="pick",
        limit=40,
        moved=20 << 20,
    )
    sent = call(
        send_body,
        [((tok // 2, 2 * cols), bf16)] * 6,
        [part, teacher_out, *table],
        [VMEM, ANY] + [ANY] * 4,
        [pltpu.VMEM((2, 2, depth, cols), bf16), DMA((2, 2))],
        name="send",
    )
    first = [
        [across(sent[k], k) for k in range(2)],
        [across(sent[2 + k], k // 2) for k in range(4)],
    ]

    last = call(
        functools.partial(more_body, PAIRS[2]),
        [((tok // 2, 2 * cols), bf16)] * 2,
        [part, teacher_out, sent[0]],
        [VMEM, ANY, ANY],
        [pltpu.VMEM((2, 2, depth, cols), bf16), DMA((2, 2))],
        name="more",
    )

    def mid(i, *tokens):
        n = tok // PAIRS[i][0][2]
        outs = call(
            functools.partial(mid_body, PAIRS[i], len(first[i]) // 2),
            [((n, cols), bf16)] * 2,
            [part, teacher_out, *first[i], *tokens],
            [VMEM, ANY] + [VMEM] * len(first[i]) + [ANY] * len(tokens),
            [pltpu.VMEM((2, depth, cols), bf16), DMA((2,))],
            name=f"mid{i}",
        )
        return outs[0], [across(outs[k], 1 - k) for k in range(2)]

    def own(i, second, extra, outs, *tokens):
        return call(
            functools.partial(own_body, i, len(first[i]) // 2),
            outs,
            [part, place, teacher_out, *table, *first[i], *second, *extra, *tokens],
            [VMEM, VMEM, ANY] + [VMEM] * (6 + len(first[i]) + len(extra)) + [ANY] * len(tokens),
            [pltpu.VMEM((depth, cols), bf16), DMA],
            name=f"own{i}",
        )

    t, second0 = mid(0, last[0])
    along_z = gate(along_z, t, first[1][0], first[1][2])
    own_map = lax.all_gather(along_z, "y", axis=0, tiled=True).reshape(4, 4, -1, along_z.shape[1])
    t, second1 = mid(1, t)
    far = own(0, second0, (), [((tok, cols // 2), bf16)] * 2, t)
    far_z = shift(far[0], "zh", 1), shift(far[1], "zh", -1)

    normed = call(
        norm_body, [((rows, d_student), bf16)], [student_hidden, student_norm_gain, far[0]], [VMEM, VMEM, ANY], name="norm"
    )[0]
    two = call(
        two_body, [((2 * rows, d_student), bf16)], [normed, across(normed, 0)], [VMEM, VMEM], name="two"
    )[0]
    near = own(1, second1, far_z, [((tok, cols), bf16)] * 2, two)
    near_z = shift(near[0], "zh", 1), shift(near[1], "zh", -1)
    last = call(
        lambda *refs: None,
        [((tok // 2, 2 * cols), bf16)] * 2,
        [*last, near[0]],
        [VMEM, VMEM, ANY],
        name="release",
        aliases={0: 0, 1: 1},
    )
    first.append([across(last[k], k) for k in range(2)])
    t, second2 = mid(2, near[0])
    every = call(
        functools.partial(every_body, feature_map.shape[0]),
        [((tok, d_wide), bf16)],
        [two, across(two, 1), t],
        [VMEM, VMEM, ANY],
        [pltpu.VMEM((tok, d_wide), f32)],
        name="every",
    )[0]
    pre, square = own(2, second2, near_z, [((tok, cols), f32), ((tok, 1), f32)], every)
    own_map = gate(own_map, square)
    other_map = lax.ppermute(own_map, "group", [(0, 1), (1, 0)])
    squares = [square] + [shift(square, "x", k) for k in (1, 2, 3)]
    mapped = mapped_half(every, own_map, square)
    backs = call(
        back_body,
        [((rows, d_student), bf16)] * 4,
        [every, mapped, pre, teacher_gain, *squares, own_map, other_map],
        [VMEM] * 8 + [ANY, VMEM],
        [
            pltpu.VMEM((4 * own_map.shape[3], tok), bf16),
            pltpu.VMEM((2, tok, d_student // 2), f32),
            pltpu.VMEM(own_map.shape, bf16),
            DMA,
        ],
        name="back",
        limit=32,
    )
    parts = [backs[0]] + [shift(backs[k], "x", k) for k in (1, 2, 3)]
    return call(
        final_body,
        [((rows, d_student), f32)],
        [student_hidden, student_norm_gain, *parts],
        [VMEM] * 6,
        name="final",
    )[0]


def solution(mesh):
    axes = ("group", "zl", "y", "x", "zh")
    fine = Mesh(mesh.devices.reshape(2, 2, 4, 4, 4), axes)
    gd, mp = ("group", "zl", "y"), ("x", "zh")
    in_specs = (
        P(gd, None, None, mp),
        P(gd),
        P(mp, None),
        P(axes, None),
        P(),
        P(axes, None),
        P(),
        P(gd, mp),
        P(gd, None),
    )
    return jax.shard_map(
        shards, mesh=fine, in_specs=in_specs, out_specs=P(axes, None), check_vma=False
    )
```

```python
import functools
import jax
import jax.numpy as jnp
from jax import lax
from jax.experimental import pallas as pl
from jax.experimental.pallas import tpu as pltpu
from jax.sharding import Mesh, PartitionSpec as P

eps = 1e-06
f32, bf16 = jnp.float32, jnp.bfloat16
VMEM = pl.BlockSpec(memory_space=pltpu.VMEM)
SMEM = pl.BlockSpec(memory_space=pltpu.SMEM)
ANY = pl.BlockSpec(memory_space=pl.ANY)
HBM = pl.BlockSpec(memory_space=pltpu.HBM)
DMA = pltpu.SemaphoreType.DMA
OFFSETS = (2, 1, 3, 0)
PAD = 512
PAIRS = (((0, 0, 2), (0, 1, 2)), ((1, 0, 1), (2, 0, 1)), ((3, 0, 2), (3, 1, 2)))


def shift(a, axis, by):
    return lax.ppermute(a, axis, [(i, (i + by) % 4) for i in range(4)])


def across(a, kind):
    return lax.ppermute(a, "x", [(i, 3 - i if kind else i ^ 1) for i in range(4)])


def partner(x, kind):
    return 3 - x if kind else x + 1 - 2 * lax.rem(x, 2)


def dot(a, b):
    return jnp.dot(a, b, preferred_element_type=f32)


def call(body, outs, ins, specs, scratch=(), name=None, aliases=None, out_spec=VMEM, limit=20, moved=1):
    return pl.pallas_call(
        body,
        out_shape=[jax.ShapeDtypeStruct(s, t) for s, t in outs],
        in_specs=specs,
        out_specs=[out_spec] * len(outs),
        scratch_shapes=list(scratch),
        compiler_params=pltpu.CompilerParams(vmem_limit_bytes=limit * 1024 * 1024),
        cost_estimate=pl.CostEstimate(flops=1, bytes_accessed=moved, transcendentals=0),
        input_output_aliases=aliases or {},
        name=name,
    )(*ins)


def gate(a, *tokens):
    return call(
        lambda *refs: None,
        [(a.shape, a.dtype)],
        [a, *tokens],
        [ANY] * (1 + len(tokens)),
        name="gate",
        aliases={0: 0},
        out_spec=ANY,
    )[0]


def column(w_ref, index, cols, buf, sem):
    start = pl.multiple_of(index * cols, cols)
    return pltpu.make_async_copy(w_ref.at[:, pl.ds(start, cols)], buf, sem)


def chunk(part_ref, where):
    q, at, of = where
    n = part_ref.shape[1] // of
    return part_ref[q, at * n : (at + 1) * n, :]


def prep_body(residual, *outs):
    x = lax.axis_index("x")
    cols = residual.shape[1] // 4
    for k, out in enumerate(outs):
        start = pl.multiple_of(lax.rem(x + k, 4) * cols, cols)
        out[...] = residual[:, pl.ds(start, cols)]


def norm_body(hidden, gain, token, out):
    rows = hidden[...].astype(f32)
    rstd = lax.rsqrt(jnp.mean(rows * rows, axis=1, keepdims=True) + eps)
    out[...] = (rows * rstd * gain[...][None, :]).astype(bf16)


def two_body(mine, came, *refs):
    out = refs[-1]
    n = mine.shape[0]
    low = lax.rem(lax.axis_index("x"), 2)
    out[pl.ds(pl.multiple_of(low * n, n), n), :] = mine[...]
    out[pl.ds(pl.multiple_of((1 - low) * n, n), n), :] = came[...]


def every_body(run, mine, came, token, out, wide):
    n = mine.shape[0]
    pad = out.shape[1] // 8
    low = lax.axis_index("x") // 2
    wide[...] = jnp.zeros_like(wide)
    for src, at in ((mine, low), (came, 1 - low)):
        here = pl.ds(pl.multiple_of(at * n, n), n)
        rows = src[...].astype(f32)
        for core in range(2):
            for y in range(4):
                for zl in range(2):
                    first = ((core * 2 + zl) * 4 + y) * run
                    to = (core * 4 + y) * pad + zl * run
                    wide[here, to : to + run] = rows[:, first : first + run]
    out[...] = wide[...].astype(bf16)


def send_blocks(part_ref, pair, wbuf, copies, outs):
    cols = wbuf.shape[-1]
    tile = cols // 4
    for kind in range(2):
        rows = chunk(part_ref, pair[kind])
        n = outs[kind][0].shape[0]
        for h in range(2):
            if copies:
                copies[kind][h].wait()
            for c in range(4):
                out = dot(rows, wbuf[kind, h, :, c * tile : (c + 1) * tile]).astype(bf16)
                for i, to in enumerate(outs[kind]):
                    to[:, h * cols + c * tile : h * cols + (c + 1) * tile] = out[i * n : (i + 1) * n]


def stacked(pieces, cs):
    return jnp.concatenate([r[:, cs].astype(f32) for r in pieces], axis=0)


def send_copies(w_ref, wbuf, sems, cols):
    x = lax.axis_index("x")
    copies = []
    for kind in range(2):
        p = partner(x, kind)
        copies.append(
            [column(w_ref, b, cols, wbuf.at[kind, h], sems.at[kind, h]) for h, b in enumerate((p, partner(p, 1 - kind)))]
        )
        for c in copies[-1]:
            c.start()
    return copies


def pick_body(sizes, ctx_ref, picks_ref, pos_ref, w_ref, token, part_ref, place_ref, w_out, picked, nat, sems):
    prompts, resp, rows = sizes
    x, z = lax.axis_index("x"), lax.axis_index("zh")
    tokens = prompts * resp
    copies = []
    for p in range(prompts):
        copies.append(
            pltpu.make_async_copy(
                ctx_ref.at[p, picks_ref[p]], picked.at[pl.ds(p * resp, resp), :], sems.at[p]
            )
        )
        copies[-1].start()
    wcopy = pltpu.make_async_copy(w_ref, w_out, sems.at[prompts])
    wcopy.start()
    lanes = min(128, tokens)
    want = jnp.broadcast_to(pos_ref[...], (lanes, tokens)).T
    lane = lax.broadcasted_iota(jnp.int32, (tokens, lanes), 1)
    chooses = [(want == lane + c * lanes).astype(bf16) for c in range(tokens // lanes)]
    slot = lax.broadcasted_iota(jnp.int32, (tokens, 4 * rows), 1)
    row = (lax.rem(x - slot // rows + 4, 4) * 4 + z) * rows + lax.rem(slot, rows)
    nat[:, : 4 * rows] = (want[:, : 4 * rows] == row).astype(f32)

    def sort(to, width):
        for q, by in enumerate(OFFSETS):
            zq = lax.rem(z + by, 4)
            for k in range(4):
                at = pl.ds(pl.multiple_of(k * 4 * rows + zq * rows, rows), rows)
                to[q, k * rows : (k + 1) * rows, :] = nat[at, :width].astype(bf16)

    sort(place_ref, 4 * rows)
    for c in copies:
        c.wait()
    nat[...] = dot(jnp.concatenate(chooses, axis=1), picked[...])
    sort(part_ref, nat.shape[1])
    wcopy.wait()


def send_body(part_ref, w_ref, *refs):
    outs, (wbuf, wsems) = refs[-8:-2], refs[-2:]
    copies = send_copies(w_ref, wbuf, wsems, outs[0].shape[1] // 2)
    send_blocks(part_ref, PAIRS[0], wbuf, copies, (outs[:1], outs[1:2]))
    send_blocks(part_ref, PAIRS[1], wbuf, None, (outs[2:4], outs[4:6]))


def more_body(pair, part_ref, w_ref, *refs):
    out_a, out_b, wbuf, wsems = refs[-4:]
    copies = send_copies(w_ref, wbuf, wsems, out_a.shape[1] // 2)
    send_blocks(part_ref, pair, wbuf, copies, ((out_a,), (out_b,)))


def mid_body(pair, pieces, part_ref, w_ref, *refs):
    out_a, out_b, wbuf, sems = refs[-4:]
    x = lax.axis_index("x")
    cols = out_a.shape[1]
    copies = [column(w_ref, partner(x, 1 - k), cols, wbuf.at[k], sems.at[k]) for k in range(2)]
    for c in copies:
        c.start()
    tile = cols // 4
    for kind, to in enumerate((out_a, out_b)):
        rows = chunk(part_ref, pair[kind])
        came = refs[kind * pieces : (kind + 1) * pieces]
        copies[kind].wait()
        for c in range(4):
            at = slice(c * tile, (c + 1) * tile)
            out = dot(rows, wbuf[kind, :, at]) + stacked(came, slice(cols + c * tile, cols + (c + 1) * tile))
            to[:, at] = out.astype(bf16)


def own_body(stage, pieces, part_ref, place_ref, w_ref, t0, t1, t2, t3, *refs):
    firsts = refs[:pieces], refs[pieces : 2 * pieces]
    seconds, refs = refs[2 * pieces : 2 * pieces + 2], refs[2 * pieces + 2 :]
    wbuf, sem = refs[-2:]
    x = lax.axis_index("x")
    cols = t0.shape[1]
    wcopy = column(w_ref, x, cols, wbuf, sem)
    wcopy.start()
    wcopy.wait()
    tile = cols // 4
    for kind, (first, second) in enumerate(zip(firsts, seconds, strict=True)):
        _, at, of = PAIRS[stage][kind]
        rows = chunk(part_ref, PAIRS[stage][kind])
        place = chunk(place_ref, PAIRS[stage][kind])
        n = rows.shape[0]
        square = jnp.zeros((n, 1), f32)
        here = slice(at * n, (at + 1) * n)
        for c in range(4):
            cs = slice(c * tile, (c + 1) * tile)
            near = slice((c % 2) * tile, (c % 2 + 1) * tile)
            table = jnp.concatenate([t[:, cs] for t in (t0, t1, t2, t3)], axis=0)
            out = dot(rows, wbuf[:, cs]) + dot(place, table)
            out += stacked(first, cs) + second[:, cs].astype(f32)
            if stage == 0:
                refs[-4 + c // 2][here, near] = out.astype(bf16)
            elif stage == 1:
                if kind == c // 2:
                    out += refs[kind][:, near].astype(f32)
                refs[-4 + kind][:, cs] = out.astype(bf16)
            else:
                out += refs[0][here, cs].astype(f32) + refs[1][here, cs].astype(f32)
                refs[-4][here, cs] = out
                square += jnp.sum(out * out, axis=1, keepdims=True)
        if stage == 2:
            refs[-3][here, :] = square


def half_start(every, half):
    g = lax.axis_index("group")
    width = every.shape[1] // 2
    return pl.multiple_of((g if half == 0 else 1 - g) * width, width)


def map_rows(every, start, maps, c):
    pad, run = every.shape[1] // 8, maps.shape[2]
    got = 0.0
    for y in range(4):
        rows = every[:, pl.ds(pl.multiple_of(start + y * pad, pad), pad)][:, :run]
        got += dot(rows, maps[y, c])
    return got


def map_body(every, maps, token, out):
    out[...] = map_rows(every, half_start(every, 0), maps, 0)


def mapped_half(every, maps, token):
    tok, cols = every.shape[0], maps.shape[3]
    return pl.pallas_call(
        map_body,
        grid=(4,),
        out_shape=jax.ShapeDtypeStruct((tok, 4 * cols), f32),
        in_specs=[
            pl.BlockSpec(every.shape, lambda c: (0, 0)),
            pl.BlockSpec((4, 1, *maps.shape[2:]), lambda c: (0, c, 0, 0)),
            ANY,
        ],
        out_specs=pl.BlockSpec((tok, cols), lambda c: (0, c)),
        compiler_params=pltpu.CompilerParams(vmem_limit_bytes=20 * 1024 * 1024),
        cost_estimate=pl.CostEstimate(flops=1, bytes_accessed=1, transcendentals=0),
        name="mapped",
    )(every, maps, token)


def back_body(every, mapped, pre, gain, s0, s1, s2, s3, own_ref, other, o0, o1, o2, o3, flipped, whole, own, sem):
    x, g = lax.axis_index("x"), lax.axis_index("group")
    fetch = pltpu.make_async_copy(own_ref, own, sem)
    fetch.start()
    cols, run = own.shape[3], own.shape[2] // 2
    total = s0[...] + s1[...] + s2[...] + s3[...]
    inverse = lax.rsqrt(total / (16 * cols) + eps)
    start = half_start(every, 1)
    for c in range(4):
        cs = slice(c * cols, (c + 1) * cols)
        gains = gain[pl.ds(pl.multiple_of((x * 4 + c) * cols, cols), cols)]
        aligned = (pre[:, cs] * inverse * gains[None, :]).astype(bf16)
        full = mapped[:, cs] + map_rows(every, start, other, c)
        flipped[cs, :] = (full - aligned.astype(f32)).T.astype(bf16)
    for i, maps in enumerate((other, own)):
        if i == 1:
            fetch.wait()
        for y in range(4):
            got = 0.0
            for c in range(4):
                got += dot(maps[y, c], flipped[c * cols : (c + 1) * cols, :])
            got = got.T
            for zl in range(2):
                to = (zl * 4 + y) * run
                whole[i, :, to : to + run] = got[:, zl * run : (zl + 1) * run]
    rows, width = o0.shape[0], whole.shape[2]
    for k, out in enumerate((o0, o1, o2, o3)):
        at = pl.ds(pl.multiple_of(lax.rem(x + k, 4) * rows, rows), rows)
        for i, core in enumerate((1 - g, g)):
            out[:, pl.ds(pl.multiple_of(core * width, width), width)] = whole[i, at, :].astype(bf16)


def final_body(hidden, gain, p0, p1, p2, p3, out):
    rows = hidden[...].astype(f32)
    rstd = lax.rsqrt(jnp.mean(rows * rows, axis=1, keepdims=True) + eps)
    xhat = rows * rstd
    summed = (p0[...].astype(f32) + p1[...].astype(f32)) + (p2[...].astype(f32) + p3[...].astype(f32))
    scaled = summed * gain[...][None, :]
    out[...] = rstd * (scaled - xhat * jnp.mean(scaled * xhat, axis=1, keepdims=True))


def shards(
    contexts,
    picks,
    teacher_out,
    teacher_residual,
    teacher_gain,
    student_hidden,
    student_norm_gain,
    feature_map,
    positions,
):
    prompts, _, resp, depth = contexts.shape
    cols = teacher_out.shape[1] // 4
    rows, d_student = student_hidden.shape
    tok = 4 * rows
    d_wide = 8 * PAD

    along_z = lax.all_gather(feature_map, ("zh", "zl"), axis=0, tiled=True)

    prepared = call(
        prep_body,
        [((rows, cols), bf16)] * 4,
        [teacher_residual],
        [VMEM],
        name="prep",
        moved=4 << 20,
    )
    table = [prepared[0]] + [shift(prepared[k], "x", k) for k in (1, 2, 3)]
    part, place, teacher_out = call(
        functools.partial(pick_body, (prompts, resp, rows)),
        [((4, tok, depth), bf16), ((4, tok, tok), bf16), (teacher_out.shape, bf16)],
        [contexts, picks, positions, teacher_out, prepared[0]],
        [HBM, SMEM, VMEM, HBM, ANY],
        [
            pltpu.VMEM((prompts * resp, depth), bf16),
            pltpu.VMEM((prompts * resp, depth), f32),
            DMA((prompts + 1,)),
        ],
        name="pick",
        limit=40,
        moved=20 << 20,
    )
    sent = call(
        send_body,
        [((tok // 2, 2 * cols), bf16)] * 6,
        [part, teacher_out, *table],
        [VMEM, ANY] + [ANY] * 4,
        [pltpu.VMEM((2, 2, depth, cols), bf16), DMA((2, 2))],
        name="send",
    )
    first = [
        [across(sent[k], k) for k in range(2)],
        [across(sent[2 + k], k // 2) for k in range(4)],
    ]

    last = call(
        functools.partial(more_body, PAIRS[2]),
        [((tok // 2, 2 * cols), bf16)] * 2,
        [part, teacher_out, sent[0]],
        [VMEM, ANY, ANY],
        [pltpu.VMEM((2, 2, depth, cols), bf16), DMA((2, 2))],
        name="more",
    )

    def mid(i, *tokens):
        n = tok // PAIRS[i][0][2]
        outs = call(
            functools.partial(mid_body, PAIRS[i], len(first[i]) // 2),
            [((n, cols), bf16)] * 2,
            [part, teacher_out, *first[i], *tokens],
            [VMEM, ANY] + [VMEM] * len(first[i]) + [ANY] * len(tokens),
            [pltpu.VMEM((2, depth, cols), bf16), DMA((2,))],
            name=f"mid{i}",
        )
        return outs[0], [across(outs[k], 1 - k) for k in range(2)]

    def own(i, second, extra, outs, *tokens):
        return call(
            functools.partial(own_body, i, len(first[i]) // 2),
            outs,
            [part, place, teacher_out, *table, *first[i], *second, *extra, *tokens],
            [VMEM, VMEM, ANY] + [VMEM] * (6 + len(first[i]) + len(extra)) + [ANY] * len(tokens),
            [pltpu.VMEM((depth, cols), bf16), DMA],
            name=f"own{i}",
        )

    t, second0 = mid(0, last[0])
    along_z = along_z + (t[0, 0] + first[1][0][0, 0] + first[1][2][0, 0]) * 0
    own_map = lax.all_gather(along_z, "y", axis=0, tiled=True).reshape(4, 4, -1, along_z.shape[1])
    t, second1 = mid(1, t)
    far = own(0, second0, (), [((tok, cols // 2), bf16)] * 2, t)
    far_z = shift(far[0], "zh", 1), shift(far[1], "zh", -1)

    normed = call(
        norm_body, [((rows, d_student), bf16)], [student_hidden, student_norm_gain, far[0]], [VMEM, VMEM, ANY], name="norm"
    )[0]
    two = call(
        two_body, [((2 * rows, d_student), bf16)], [normed, across(normed, 0)], [VMEM, VMEM], name="two"
    )[0]
    near = own(1, second1, far_z, [((tok, cols), bf16)] * 2, two)
    near_z = shift(near[0], "zh", 1), shift(near[1], "zh", -1)
    last = call(
        lambda *refs: None,
        [((tok // 2, 2 * cols), bf16)] * 2,
        [*last, near[0]],
        [VMEM, VMEM, ANY],
        name="release",
        aliases={0: 0, 1: 1},
    )
    first.append([across(last[k], k) for k in range(2)])
    t, second2 = mid(2, near[0])
    every = call(
        functools.partial(every_body, feature_map.shape[0]),
        [((tok, d_wide), bf16)],
        [two, across(two, 1), t],
        [VMEM, VMEM, ANY],
        [pltpu.VMEM((tok, d_wide), f32)],
        name="every",
    )[0]
    pre, square = own(2, second2, near_z, [((tok, cols), f32), ((tok, 1), f32)], every)
    own_map = gate(own_map, square)
    other_map = lax.ppermute(own_map, "group", [(0, 1), (1, 0)])
    squares = [square] + [shift(square, "x", k) for k in (1, 2, 3)]
    mapped = mapped_half(every, own_map, square)
    backs = call(
        back_body,
        [((rows, d_student), bf16)] * 4,
        [every, mapped, pre, teacher_gain, *squares, own_map, other_map],
        [VMEM] * 8 + [ANY, VMEM],
        [
            pltpu.VMEM((4 * own_map.shape[3], tok), bf16),
            pltpu.VMEM((2, tok, d_student // 2), f32),
            pltpu.VMEM(own_map.shape, bf16),
            DMA,
        ],
        name="back",
        limit=32,
    )
    parts = [backs[0]] + [shift(backs[k], "x", k) for k in (1, 2, 3)]
    return call(
        final_body,
        [((rows, d_student), f32)],
        [student_hidden, student_norm_gain, *parts],
        [VMEM] * 6,
        name="final",
    )[0]


def solution(mesh):
    axes = ("group", "zl", "y", "x", "zh")
    fine = Mesh(mesh.devices.reshape(2, 2, 4, 4, 4), axes)
    gd, mp = ("group", "zl", "y"), ("x", "zh")
    in_specs = (
        P(gd, None, None, mp),
        P(gd),
        P(mp, None),
        P(axes, None),
        P(),
        P(axes, None),
        P(),
        P(gd, mp),
        P(gd, None),
    )
    return jax.shard_map(
        shards, mesh=fine, in_specs=in_specs, out_specs=P(axes, None), check_vma=False
    )
```
